32 devices in a mesh: prompt: 8 (over z, core), resp: 4 (over y, x).
Axes of the slice: x: 2, y: 2, z: 4, core: 2. Of those that a mesh axis runs over, the one named last changes fastest.
Arguments:
- inputs: bfloat16 [32, 128, 16384], P(('prompt', 'resp')), parts along dimension 0, may hold values from -6 to 6
- cotangent: bfloat16 [32, 128, 16384], P(('prompt', 'resp')), parts along dimension 0, may hold values from -96 to 96
- b_proj: bfloat16 [32, 128, 2048], P(('prompt', 'resp')), parts along dimension 0, may hold values from -0.375 to 0.375
- c_proj: bfloat16 [32, 128, 2048], P(('prompt', 'resp')), parts along dimension 0, may hold values from -0.375 to 0.375
- dt_raw: float32 [32, 128, 256], P(('prompt', 'resp')), parts along dimension 0, may hold values from -6 to 6
- decay_rate: float32 [256], replicated, may hold values from 0.003 to 0.06
- state_codes: bfloat16 [2048, 64, 256], P(('prompt', 'resp')), parts along dimension 0, may hold values from -6 to 6
- state_scales: bfloat16 [2048, 64], P(('prompt', 'resp')), parts along dimension 0, may hold values from 0.25 to 2
- sign_bucket: int32 [32], P(('prompt', 'resp')), parts along dimension 0, may hold values from 0 to 1
- adv_scale: float32 [32], P(('prompt', 'resp')), parts along dimension 0, may hold values from 0.5 to 2
- lengths: int32 [32], P(('prompt', 'resp')), parts along dimension 0, may hold values from 64 to 128, as said below
Outputs:
- grad_state: float32 [2048, 64, 256], P(('prompt', 'resp')), parts along dimension 0
- grad_b: bfloat16 [32, 128, 2048], P(('prompt', 'resp')), parts along dimension 0
- grad_c: bfloat16 [32, 128, 2048], P(('prompt', 'resp')), parts along dimension 0
- grad_dt: float32 [32, 128, 256], P(('prompt', 'resp')), parts along dimension 0
The draws below stay inside these ranges and needn't reach their ends.
There are 8 independent parts, one for each index of `prompt`. The reference program is written for one: setup_inputs(seed, part) draws one part's arguments, and reference() takes and returns one part's arrays. A program takes and returns all parts, laid end to end along the dimension named above; an argument that names none is the same for every part. Nothing has to cross between parts.
Inputs may be any that keep to these rules, and one draw needn't show every extreme that they name: `lengths`: every response has at least 64 valid tokens; some response of each prompt has exactly 128.
All inputs are finite; a program needn't handle non-finite values.
Results may differ from the reference program's by a relative error of at most 0.001.
Values may be sent and summed in bfloat16 or wider, within the bound.
A program may use at most 128 MiB of HBM per device.

```python
import math
import jax
import jax.numpy as jnp
from jax import lax

H = 256
P_SIZE = 64
N = 256
G = 8
TOK = 128
RESP = 4


def draw_lengths(key, part):
    key = jax.random.fold_in(key, 11)
    first_key, second_key = jax.random.split(key)
    values = jax.random.randint(first_key, (RESP,), TOK // 2, TOK + 1)
    chosen = jax.random.randint(second_key, (), 0, RESP)
    return jnp.where(jnp.arange(RESP) == chosen, TOK, values).astype(jnp.int32)


def with_ends(drawn, stream_key, least, largest):
    longest = drawn.shape.index(max(drawn.shape))
    spots = []
    for shift in (0, 1):
        where = [jax.random.randint(jax.random.fold_in(stream_key, axis), (), 0, length) for axis, length in enumerate(drawn.shape)]
        where[longest] = (where[longest] + shift) % drawn.shape[longest]
        spots.append(tuple(where))
    return drawn.at[spots[0]].set(least).at[spots[1]].set(largest)


def level_of(key, shape, pieces, least, largest):
    level = 1.0
    for position, blocks in pieces:
        draws = jax.random.uniform(jax.random.fold_in(jax.random.fold_in(key, 6), position), (blocks,), jnp.float32, least / len(pieces), largest / len(pieces))
        level = level * jnp.repeat(jnp.exp(draws), shape[position] // blocks).reshape((-1,) + (1,) * (len(shape) - 1 - position))
    return level


def gaussian(key, extent, deviation, most, pieces=(), held_as=jnp.bfloat16):
    array = deviation * jax.random.normal(key, extent, jnp.float32)
    if pieces:
        array = array * level_of(key, extent, pieces, -0.22, 0.18)
    return jnp.clip(array, -most, most).astype(held_as)


def setup_inputs(seed: int = 0, part: int = 0) -> dict:
    keys = jax.random.split(jax.random.key(seed), 12)
    part_keys = jax.random.split(jax.random.fold_in(keys[11], part), 12)
    return {
        "inputs": gaussian(part_keys[0], (RESP, TOK, H * P_SIZE), 1.0, 6.0, ((0, 4),)),
        "cotangent": gaussian(part_keys[1], (RESP, TOK, H * P_SIZE), 16.0, 96.0, ((0, 4),)),
        "b_proj": gaussian(part_keys[2], (RESP, TOK, G * N), N ** -0.5, 0.375, ((0, 4),)),
        "c_proj": gaussian(part_keys[3], (RESP, TOK, G * N), N ** -0.5, 0.375, ((0, 4),)),
        "dt_raw": gaussian(part_keys[4], (RESP, TOK, H), 1.0, 6.0, ((0, 4),), jnp.float32),
        "decay_rate": jnp.clip(jnp.exp(jax.random.uniform(keys[5], (H,), jnp.float32, math.log(0.003), math.log(0.06))), 0.003, 0.06),
        "state_codes": gaussian(part_keys[6], (H, P_SIZE, N), 1.0, 6.0, ((0, 4),)),
        "state_scales": jnp.clip(jnp.exp(math.log(2.0) - 2.0794415 * jax.random.uniform(part_keys[7], (H, P_SIZE), jnp.float32) ** level_of(part_keys[7], (H, P_SIZE), ((0, 4),), -0.2, 0.2)), 0.25, 2.0).astype(jnp.bfloat16),
        "sign_bucket": with_ends(jax.random.randint(part_keys[8], (RESP,), 0, 2), jax.random.fold_in(part_keys[8], 1), 0, 1).astype(jnp.int32),
        "adv_scale": jnp.clip(jnp.exp(math.log(2.0) - 1.3862944 * jax.random.uniform(part_keys[9], (RESP,), jnp.float32) ** level_of(part_keys[9], (RESP,), ((0, 4),), -0.2, 0.2)), 0.5, 2.0),
        "lengths": draw_lengths(jax.random.fold_in(jax.random.fold_in(keys[11], part), 71), part),
    }


def group_forward(group_x, scores, group_c, group_dt, group_rate, group_state):
    tok_rows = group_x.shape[0]
    head_count = group_dt.shape[1]
    step_size = jax.nn.softplus(group_dt)
    log_decay = jnp.cumsum(-step_size * group_rate[None, :], axis=0)
    decay_rows = log_decay.T
    decay_gap = decay_rows[:, :, None] - decay_rows[:, None, :]
    causal = jnp.arange(tok_rows, dtype=jnp.int32)[:, None] >= jnp.arange(tok_rows, dtype=jnp.int32)[None, :]
    attenuation = jnp.where(causal[None], jnp.exp(jnp.where(causal[None], decay_gap, 0.0)), 0.0)
    mixing = attenuation * scores[None] * step_size.T[:, None, :]
    head_x = group_x.reshape(tok_rows, head_count, -1)
    within = jnp.einsum('hts,shp->thp', mixing, head_x, precision=lax.Precision.HIGHEST)
    carried = jnp.exp(log_decay)[:, :, None] * jnp.einsum('tn,hpn->thp', group_c, group_state, precision=lax.Precision.HIGHEST)
    return (within + carried).reshape(tok_rows, -1)

def response_grads(x_rows, up_rows, b_rows, c_rows, dt_rows, rate, prefix_state, row_coef, with_state):
    state_dim = prefix_state.shape[2]
    head_dim = prefix_state.shape[1]
    group_count = b_rows.shape[1] // state_dim
    group_heads = rate.shape[0] // group_count
    group_width = group_heads * head_dim
    tok_rows = x_rows.shape[0]

    def one_group(group_idx):
        group_x = lax.dynamic_slice_in_dim(x_rows, group_idx * group_width, group_width, 1).astype(jnp.float32)
        group_dy = lax.dynamic_slice_in_dim(up_rows, group_idx * group_width, group_width, 1).astype(jnp.float32) * row_coef[:, None]
        b_half = lax.dynamic_slice_in_dim(b_rows, group_idx * state_dim, state_dim, 1)
        c_half = lax.dynamic_slice_in_dim(c_rows, group_idx * state_dim, state_dim, 1)
        group_b = b_half.astype(jnp.float32)
        group_c = c_half.astype(jnp.float32)
        scores = jnp.dot(c_half, b_half.T, preferred_element_type=jnp.float32)
        group_dt = lax.dynamic_slice_in_dim(dt_rows, group_idx * group_heads, group_heads, 1)
        group_rate = lax.dynamic_slice_in_dim(rate, group_idx * group_heads, group_heads, 0)
        group_state = lax.dynamic_slice_in_dim(prefix_state, group_idx * group_heads, group_heads, 0)
        if with_state:

            def forward(s_in, c_in, dt_in, state_in):
                return group_forward(group_x, s_in, c_in, dt_in, group_rate, state_in)
            result, pullback = jax.vjp(forward, scores, group_c, group_dt, group_state)
        else:

            def forward(s_in, c_in, dt_in):
                return group_forward(group_x, s_in, c_in, dt_in, group_rate, group_state)
            result, pullback = jax.vjp(forward, scores, group_c, group_dt)
        grads = pullback(group_dy)
        d_scores = grads[0]
        grad_b = jnp.dot(d_scores.T, group_c, precision=lax.Precision.HIGHEST)
        grad_c = jnp.dot(d_scores, group_b, precision=lax.Precision.HIGHEST) + grads[1]
        return (grad_b, grad_c) + tuple(grads[2:])
    results = lax.map(one_group, jnp.arange(group_count, dtype=jnp.int32))
    grad_b = results[0].transpose(1, 0, 2).reshape(tok_rows, -1)
    grad_c = results[1].transpose(1, 0, 2).reshape(tok_rows, -1)
    grad_dt = results[2].transpose(1, 0, 2).reshape(tok_rows, -1)
    if with_state:
        return (grad_b, grad_c, grad_dt, results[3].reshape(rate.shape[0], head_dim, state_dim))
    return (grad_b, grad_c, grad_dt)

def reference(inputs, cotangent, b_proj, c_proj, dt_raw, decay_rate, state_codes, state_scales, sign_bucket, adv_scale, lengths):
    prefix_state = state_codes.astype(jnp.float32) * state_scales.astype(jnp.float32)[:, :, None]
    positions = jnp.arange(TOK, dtype=jnp.int32)

    def per_response(resp_idx):
        sign_value = 2.0 * sign_bucket[resp_idx].astype(jnp.float32) - 1.0
        coefficient = sign_value * adv_scale[resp_idx] / lengths[resp_idx].astype(jnp.float32)
        row_coef = jnp.where(positions < lengths[resp_idx], coefficient, jnp.zeros((), jnp.float32))
        return response_grads(inputs[resp_idx], cotangent[resp_idx], b_proj[resp_idx], c_proj[resp_idx], dt_raw[resp_idx], decay_rate, prefix_state, row_coef, True)
    grad_b, grad_c, grad_dt, grad_parts = lax.map(per_response, jnp.arange(RESP, dtype=jnp.int32))
    return (lax.optimization_barrier(jnp.sum(grad_parts, axis=0)), grad_b.astype(jnp.bfloat16), grad_c.astype(jnp.bfloat16), grad_dt)
```

```python
import functools
import jax
import jax.numpy as jnp
from jax import lax
from jax.experimental import pallas as pl
from jax.experimental.pallas import tpu as pltpu
from jax.sharding import PartitionSpec as P

F32 = jnp.float32
BF16 = jnp.bfloat16
CHUNK = 512
VMEM_BYTES = 48 * 1024 * 1024


def dot(left, right):
    return lax.dot_general(left, right, (((1,), (0,)), ((), ())), preferred_element_type=F32)


def dot_nt(left, right):
    return lax.dot_general(left, right, (((1,), (1,)), ((), ())), preferred_element_type=F32)


def dot_tn(left, right):
    return lax.dot_general(left, right, (((0,), (0,)), ((), ())), preferred_element_type=F32)


def split(value):
    high = value.astype(BF16)
    return high, (value - high.astype(F32)).astype(BF16)


def three_parts(value):
    high = value.astype(BF16)
    rest = value - high.astype(F32)
    middle, low = split(rest)
    return jnp.concatenate([high, middle, low], axis=1)


def head_spread(heads, head_dim, start, width):
    row = lax.broadcasted_iota(jnp.int32, (heads, width), 0)
    col = lax.broadcasted_iota(jnp.int32, (heads, width), 1) + start
    first = row * head_dim
    one = jnp.where((col >= first) & (col < first + head_dim), 1.0, 0.0).astype(BF16)
    return jnp.concatenate([one, one, one], axis=0)


def head_gather(heads, head_dim, start, width):
    row = lax.broadcasted_iota(jnp.int32, (width, heads), 0) + start
    first = lax.broadcasted_iota(jnp.int32, (width, heads), 1) * head_dim
    return jnp.where((row >= first) & (row < first + head_dim), 1.0, 0.0).astype(BF16)


def within_kernel(
    head_dim, x_ref, d_ref, b_ref, c_ref, wa_ref, wb_ref, gb_ref, gc_ref, row_ref, col_ref, spread, gather
):
    heads = wa_ref.shape[2]
    tok, width = x_ref.shape
    chunk = min(CHUNK, width)

    @pl.when(pl.program_id(0) == 0)
    def _():
        spread[...] = head_spread(heads, head_dim, 0, width)
        gather[...] = head_gather(heads, head_dim, 0, width)

    b = b_ref[...]
    c = c_ref[...]
    at = lax.broadcasted_iota(jnp.int32, (tok, tok), 0)
    of = lax.broadcasted_iota(jnp.int32, (tok, tok), 1)
    s_hi, s_lo = split(jnp.where(at >= of, dot_nt(c, b), 0.0))
    scores = jnp.concatenate([s_hi, s_lo, s_hi], axis=1)
    t_hi, t_lo = split(jnp.where(at <= of, dot_nt(b, c), 0.0))
    flipped = jnp.concatenate([t_hi, t_lo, t_hi], axis=1)
    wa = three_parts(wa_ref[0])
    wb = three_parts(wb_ref[0])
    d_scores = jnp.zeros((tok, tok), F32)
    sums = jnp.zeros((4 * tok, heads), F32)
    for start in range(0, width, chunk):
        here = slice(start, start + chunk)
        ex = spread[:, here]
        w = d_ref[:, here].astype(F32) * dot(wa, ex)
        x = x_ref[:, here].astype(F32) * dot(wb, ex)
        w_hi, w_lo = split(w)
        x_hi, x_lo = split(x)
        d_scores += dot_nt(
            jnp.concatenate([w_hi, w_hi, w_lo], axis=1), jnp.concatenate([x_hi, x_lo, x_hi], axis=1)
        )
        p = w * dot(scores, jnp.concatenate([x_hi, x_hi, x_lo], axis=0))
        q = x * dot(flipped, jnp.concatenate([w_hi, w_hi, w_lo], axis=0))
        sums += dot(jnp.concatenate(split(p) + split(q), axis=0), gather[here, :])
    row_ref[0] = sums[:tok] + sums[tok : 2 * tok]
    col_ref[0] = sums[2 * tok : 3 * tok] + sums[3 * tok :]
    d_scores = jnp.where(at >= of, d_scores, 0.0)
    gc_ref[...] = dot(jnp.concatenate(split(d_scores), axis=1), jnp.concatenate([b, b], axis=0))
    gb_ref[...] = dot(
        jnp.concatenate(split(d_scores.T), axis=1), jnp.concatenate([c, c], axis=0)
    ).astype(BF16)


def within(x, d, b, c, wa, wb, head_dim):
    groups, tok, heads = wa.shape
    width = heads * head_dim
    state_dim = b.shape[1] // groups
    cols = lambda g: (0, g)
    lead = lambda g: (g, 0, 0)
    return pl.pallas_call(
        functools.partial(within_kernel, head_dim),
        grid=(groups,),
        in_specs=[
            pl.BlockSpec((tok, width), cols),
            pl.BlockSpec((tok, width), cols),
            pl.BlockSpec((tok, state_dim), cols),
            pl.BlockSpec((tok, state_dim), cols),
            pl.BlockSpec((1, tok, heads), lead),
            pl.BlockSpec((1, tok, heads), lead),
        ],
        out_specs=[
            pl.BlockSpec((tok, state_dim), cols),
            pl.BlockSpec((tok, state_dim), cols),
            pl.BlockSpec((1, tok, heads), lead),
            pl.BlockSpec((1, tok, heads), lead),
        ],
        out_shape=[
            jax.ShapeDtypeStruct(b.shape, BF16),
            jax.ShapeDtypeStruct(c.shape, F32),
            jax.ShapeDtypeStruct(wa.shape, F32),
            jax.ShapeDtypeStruct(wa.shape, F32),
        ],
        scratch_shapes=[pltpu.VMEM((3 * heads, width), BF16), pltpu.VMEM((width, heads), BF16)],
        compiler_params=pltpu.CompilerParams(vmem_limit_bytes=VMEM_BYTES),
        cost_estimate=pl.CostEstimate(
            flops=24 * tok * tok * x.shape[1], bytes_accessed=4 * x.size + 6 * b.size, transcendentals=0
        ),
        name="within",
    )(x, d, b, c, wa, wb)


def carried_kernel(head_dim, d_ref, c_ref, w_ref, codes_ref, scale_ref, dc_ref, dl_ref):
    heads = w_ref.shape[2]
    tok, width = d_ref.shape
    chunk = min(CHUNK, width)
    c = c_ref[...]
    wt = three_parts(w_ref[0])
    d_c = jnp.zeros((2 * tok, c.shape[1]), F32)
    sums = jnp.zeros((2 * tok, heads), F32)
    for start in range(0, width, chunk):
        here = slice(start, start + chunk)
        codes = codes_ref[here, :]
        w = d_ref[:, here].astype(F32) * dot(wt, head_spread(heads, head_dim, start, chunk))
        w = w * scale_ref[:, here]
        d_c += dot(jnp.concatenate(split(w), axis=0), codes)
        p = w * dot_nt(c, codes)
        sums += dot(jnp.concatenate(split(p), axis=0), head_gather(heads, head_dim, start, chunk))
    dc_ref[...] = d_c[:tok] + d_c[tok:]
    dl_ref[0] = sums[:tok] + sums[tok:]


def carried(d, c, w, codes, scale, head_dim):
    span, tok, heads = w.shape
    width = heads * head_dim
    state_dim = codes.shape[1]
    cols = lambda g: (0, g)
    return pl.pallas_call(
        functools.partial(carried_kernel, head_dim),
        grid=(span,),
        in_specs=[
            pl.BlockSpec((tok, width), cols),
            pl.BlockSpec((tok, state_dim), cols),
            pl.BlockSpec((1, tok, heads), lambda g: (g, 0, 0)),
            pl.BlockSpec((width, state_dim), lambda g: (g, 0)),
            pl.BlockSpec((1, width), cols),
        ],
        out_specs=[
            pl.BlockSpec((tok, state_dim), cols),
            pl.BlockSpec((1, tok, heads), lambda g: (g, 0, 0)),
        ],
        out_shape=[
            jax.ShapeDtypeStruct((tok, span * state_dim), F32),
            jax.ShapeDtypeStruct(w.shape, F32),
        ],
        compiler_params=pltpu.CompilerParams(vmem_limit_bytes=VMEM_BYTES),
        cost_estimate=pl.CostEstimate(
            flops=6 * tok * codes.size, bytes_accessed=2 * (d.size + codes.size), transcendentals=0
        ),
        name="carried",
    )(d, c, w, codes, scale)


def state_kernel(head_dim, count, *refs):
    out_ref = refs[-1]
    chunk, state_dim = out_ref.shape
    heads = refs[2 * count].shape[2]
    per_group = heads * head_dim // chunk
    start = lax.rem(pl.program_id(0), per_group) * chunk
    spread = head_spread(heads, head_dim, start, chunk)
    total = jnp.zeros((state_dim, chunk), F32)
    for i in range(count):
        d_ref, c_ref, w_ref = refs[i], refs[count + i], refs[2 * count + i]
        w = d_ref[...].astype(F32) * dot(three_parts(w_ref[0]), spread)
        c = c_ref[...]
        total += dot_tn(jnp.concatenate([c, c], axis=0), jnp.concatenate(split(w), axis=0))
    out_ref[...] = total.T


def state_gradient(ds, cs, ws, head_dim):
    span, tok, heads = ws[0].shape
    width = ds[0].shape[1]
    chunk = min(CHUNK, heads * head_dim)
    per_group = heads * head_dim // chunk
    state_dim = cs[0].shape[1] // span
    count = len(ds)
    return pl.pallas_call(
        functools.partial(state_kernel, head_dim, count),
        grid=(width // chunk,),
        in_specs=[pl.BlockSpec((tok, chunk), lambda j: (0, j))] * count
        + [pl.BlockSpec((tok, state_dim), lambda j: (0, j // per_group))] * count
        + [pl.BlockSpec((1, tok, heads), lambda j: (j // per_group, 0, 0))] * count,
        out_specs=pl.BlockSpec((chunk, state_dim), lambda j: (j, 0)),
        out_shape=jax.ShapeDtypeStruct((width, state_dim), F32),
        compiler_params=pltpu.CompilerParams(vmem_limit_bytes=VMEM_BYTES),
        cost_estimate=pl.CostEstimate(
            flops=4 * count * tok * width * state_dim,
            bytes_accessed=2 * count * tok * width + 4 * width * state_dim,
            transcendentals=0,
        ),
        name="state_gradient",
    )(*ds, *cs, *ws)


def per_device(
    count,
    inputs,
    cotangent,
    b_proj,
    c_proj,
    dt_raw,
    decay_rate,
    state_codes,
    state_scales,
    sign_bucket,
    adv_scale,
    lengths,
):
    x, d, b, c, dt = inputs[0], cotangent[0], b_proj[0], c_proj[0], dt_raw[0]
    tok, all_heads = dt.shape
    own, head_dim, state_dim = state_codes.shape
    groups = b.shape[1] // state_dim
    group_heads = all_heads // groups
    span = max(1, own // group_heads)
    part = own // span
    width = own * head_dim
    me = lax.axis_index("resp")

    step = jax.nn.softplus(dt)
    at = jnp.arange(tok, dtype=jnp.int32)
    lower = (at[:, None] >= at[None, :]).astype(F32)
    log_decay = -decay_rate[None, :] * jnp.dot(lower, step, precision=lax.Precision.HIGHEST)
    sign_value = 2.0 * sign_bucket[0].astype(F32) - 1.0
    coefficient = sign_value * adv_scale[0] / lengths[0].astype(F32)
    row_coef = jnp.where(at < lengths[0], coefficient, jnp.zeros((), F32))
    wa = row_coef[:, None] * jnp.exp(log_decay)
    wb = step * jnp.exp(-log_decay)

    def by_group(value, pieces):
        return value.reshape(tok, pieces, -1).transpose(1, 0, 2)

    def flat(value):
        return value.transpose(1, 0, 2).reshape(tok, -1)

    def first_group(owner):
        return owner * own // group_heads

    def pieces_for(owner):
        return (
            lax.dynamic_slice_in_dim(d, owner * width, width, 1),
            lax.dynamic_slice_in_dim(c, first_group(owner) * state_dim, span * state_dim, 1),
            by_group(lax.dynamic_slice_in_dim(wa, owner * own, own, 1), span),
        )

    def swap(value, k):
        return lax.ppermute(value, "resp", [(i, i ^ k) for i in range(count)])

    received = [pieces_for(me)]
    for k in range(1, count):
        received.append(tuple(swap(piece, k) for piece in pieces_for(me ^ k)))

    grad_b, grad_c, row_sum, col_sum = within(
        x, d, b, c, by_group(wa, groups), by_group(wb, groups), head_dim
    )
    codes = state_codes.reshape(width, state_dim)
    scale = state_scales.astype(F32).reshape(1, width)
    returned = []
    for k in range(count):
        d_c, d_l = carried(*received[k], codes, scale, head_dim)
        returned.append((d_c, d_l) if k == 0 else (swap(d_c, k), swap(d_l, k)))
    ds, cs, ws = zip(*received)
    grad_state = state_gradient(ds, cs, ws, head_dim).reshape(state_codes.shape)

    d_log = jnp.zeros((tok, all_heads), F32)
    for k in range(count):
        owner = me ^ k
        d_c, d_l = returned[k]
        first = first_group(owner) * state_dim
        held = lax.dynamic_slice_in_dim(grad_c, first, span * state_dim, 1)
        grad_c = lax.dynamic_update_slice_in_dim(grad_c, held + d_c, first, 1)
        d_log = lax.dynamic_update_slice_in_dim(d_log, flat(d_l), owner * own, 1)
    row_sum, col_sum = flat(row_sum), flat(col_sum)
    d_log = d_log + (row_sum - col_sum)
    later = jnp.dot(lower.T, d_log, precision=lax.Precision.HIGHEST)
    grad_dt = (col_sum / step - decay_rate[None, :] * later) * jax.nn.sigmoid(dt)
    return grad_state, grad_b[None], grad_c.astype(BF16)[None], grad_dt[None]


def solution(mesh):
    both = ("prompt", "resp")
    return jax.shard_map(
        functools.partial(per_device, mesh.shape["resp"]),
        mesh=mesh,
        in_specs=(
            P(both, None, None),
            P(both, None, None),
            P(both, None, None),
            P(both, None, None),
            P(both, None, None),
            P(),
            P(both, None, None),
            P(both, None),
            P(both),
            P(both),
            P(both),
        ),
        out_specs=(P(both, None, None),) * 4,
        check_vma=False,
    )
```

```python
import functools
import jax
import jax.numpy as jnp
from jax import lax
from jax.experimental import pallas as pl
from jax.experimental.pallas import tpu as pltpu
from jax.sharding import PartitionSpec as P

F32 = jnp.float32
BF16 = jnp.bfloat16
CHUNK = 512
VMEM_BYTES = 56 * 1024 * 1024


def dot(left, right):
    return lax.dot_general(left, right, (((1,), (0,)), ((), ())), preferred_element_type=F32)


def dot_nt(left, right):
    return lax.dot_general(left, right, (((1,), (1,)), ((), ())), preferred_element_type=F32)


def dot_tn(left, right):
    return lax.dot_general(left, right, (((0,), (0,)), ((), ())), preferred_element_type=F32)


def split(value):
    high = value.astype(BF16)
    return high, (value - high.astype(F32)).astype(BF16)


def three_rows(value):
    high = value.astype(BF16)
    middle, low = split(value - high.astype(F32))
    return jnp.concatenate([high, middle, low], axis=0)


def head_mask(heads, head_dim, start, width):
    row = lax.broadcasted_iota(jnp.int32, (heads, width), 0)
    col = lax.broadcasted_iota(jnp.int32, (heads, width), 1) + start
    first = row * head_dim
    return jnp.where((col >= first) & (col < first + head_dim), 1.0, 0.0).astype(BF16)


def spread(weights, mask):
    return dot_tn(three_rows(weights), jnp.concatenate([mask, mask, mask], axis=0))


def kernel(
    count,
    groups,
    head_dim,
    x_hbm,
    d_hbm,
    b_ref,
    c_ref,
    dt_ref,
    rate_ref,
    codes_hbm,
    scale_ref,
    sign_ref,
    adv_ref,
    length_ref,
    state_hbm,
    gb_ref,
    gc_ref,
    gdt_ref,
    x_ref,
    d_ref,
    codes_ref,
    state_ref,
    got_d,
    got_c,
    got_w,
    parts_ref,
    c_flip,
    out_dc,
    out_dl,
    got_dc,
    got_dl,
    wa_ref,
    wb_ref,
    row_ref,
    col_ref,
    log_ref,
    total_ref,
    load_sem,
    state_sem,
    d_send,
    d_recv,
    c_send,
    c_recv,
    w_send,
    w_recv,
    dc_send,
    dc_recv,
    dl_send,
    dl_recv,
):
    tok, all_heads = dt_ref.shape
    state_dim = b_ref.shape[1] // groups
    group_heads = all_heads // groups
    group_width = group_heads * head_dim
    own = all_heads // count
    width = own * head_dim
    span = max(1, own // group_heads)
    part = own // span
    part_width = part * head_dim
    me = lax.axis_index("resp")

    def other(k):
        return lax.rem(me + k + count, count)

    def first_group(owner):
        return owner * own // group_heads

    barrier = pltpu.get_barrier_semaphore()
    for k in range(1, count):
        pl.semaphore_signal(
            barrier, inc=1, device_id={"resp": other(k)}, device_id_type=pl.DeviceIdType.MESH
        )

    def columns(owner, s):
        return pl.ds(pl.multiple_of(owner * width + s * part_width, 128), part_width)

    loads = [
        pltpu.make_async_copy(x_hbm, x_ref, load_sem.at[0]),
        pltpu.make_async_copy(d_hbm, d_ref, load_sem.at[1]),
        pltpu.make_async_copy(codes_hbm, codes_ref, load_sem.at[2]),
        pltpu.make_async_copy(
            d_hbm.at[:, pl.ds(pl.multiple_of(me * width, 128), width)], got_d.at[0], load_sem.at[3]
        ),
    ]
    for load in loads:
        load.start()
    pl.semaphore_wait(barrier, count - 1)

    def remote(source, target, send, recv, k):
        return pltpu.make_async_remote_copy(
            src_ref=source,
            dst_ref=target,
            send_sem=send,
            recv_sem=recv,
            device_id={"resp": other(k)},
            device_id_type=pl.DeviceIdType.MESH,
        )

    def send_d(k, s):
        return remote(
            d_hbm.at[:, columns(other(k), s)],
            got_d.at[k, :, pl.ds(s * part_width, part_width)],
            d_send.at[k, s],
            d_recv.at[k, s],
            k,
        )

    def state_columns(owner):
        return pl.ds(pl.multiple_of(first_group(owner) * state_dim, 128), span * state_dim)

    def heads_of(owner):
        return pl.ds(pl.multiple_of(owner * own, 8), own)

    def send_c(k):
        return remote(
            c_ref.at[:, state_columns(other(k))], got_c.at[k], c_send.at[k], c_recv.at[k], k
        )

    def send_w(k):
        return remote(wa_ref.at[heads_of(other(k)), :], got_w.at[k], w_send.at[k], w_recv.at[k], k)

    for k in range(1, count):
        send_d(k, 0).start()

    at = lax.broadcasted_iota(jnp.int32, (tok, tok), 0)
    of = lax.broadcasted_iota(jnp.int32, (tok, tok), 1)
    causal = at >= of
    lower = jnp.where(causal, 1.0, 0.0).astype(BF16)
    upper = jnp.where(at <= of, 1.0, 0.0).astype(BF16)
    dt = dt_ref[...]
    step = jnp.maximum(dt, 0.0) + jnp.log1p(jnp.exp(-jnp.abs(dt)))
    rate = rate_ref[...]
    log_decay = -rate * dot(jnp.concatenate([lower] * 3, axis=1), three_rows(step))
    sign = 2.0 * jnp.full((tok, 1), sign_ref[0], jnp.int32).astype(F32) - 1.0
    length = jnp.full((tok, 1), length_ref[0], jnp.int32)
    coefficient = sign * adv_ref[0] / length.astype(F32)
    row_coef = jnp.where(lax.broadcasted_iota(jnp.int32, (tok, 1), 0) < length, coefficient, 0.0)
    wa_ref[...] = (row_coef * jnp.exp(log_decay)).T
    wb_ref[...] = (step * jnp.exp(-log_decay)).T

    for k in range(1, count):
        send_w(k).start()
        send_c(k).start()
    for s in range(1, span):
        for k in range(1, count):
            send_d(k, s).start()
    got_c[0] = c_ref[:, state_columns(me)]
    got_w[0] = wa_ref[heads_of(me), :]
    loads[0].wait()
    loads[1].wait()

    chunk = min(CHUNK, group_width)

    def one_group(g, carry):
        states = pl.ds(pl.multiple_of(g * state_dim, 128), state_dim)
        heads = pl.ds(pl.multiple_of(g * group_heads, 8), group_heads)
        b = b_ref[:, states]
        c = c_ref[:, states]
        s_hi, s_lo = split(jnp.where(causal, dot_nt(c, b), 0.0))
        scores = jnp.concatenate([s_hi, s_lo, s_hi], axis=1)
        t_hi, t_lo = split(jnp.where(at <= of, dot_nt(b, c), 0.0))
        flipped = jnp.concatenate([t_hi, t_lo, t_hi], axis=1)
        wa = wa_ref[heads, :]
        wb = wb_ref[heads, :]
        d_scores = jnp.zeros((2 * tok, 2 * tok), F32)
        sums = jnp.zeros((group_heads, 4 * tok), F32)
        for start in range(0, group_width, chunk):
            here = pl.ds(pl.multiple_of(g * group_width + start, 128), chunk)
            mask = head_mask(group_heads, head_dim, start, chunk)
            w = d_ref[:, here].astype(F32) * spread(wa, mask)
            x = x_ref[:, here].astype(F32) * spread(wb, mask)
            w_hi, w_lo = split(w)
            x_hi, x_lo = split(x)
            d_scores += dot_nt(
                jnp.concatenate([w_hi, w_lo], axis=0), jnp.concatenate([x_hi, x_lo], axis=0)
            )
            p = w * dot(scores, jnp.concatenate([x_hi, x_hi, x_lo], axis=0))
            q = x * dot(flipped, jnp.concatenate([w_hi, w_hi, w_lo], axis=0))
            sums += dot_nt(mask, jnp.concatenate(split(p) + split(q), axis=0))
        row_ref[heads, :] = sums[:, :tok] + sums[:, tok : 2 * tok]
        col_ref[heads, :] = sums[:, 2 * tok : 3 * tok] + sums[:, 3 * tok :]
        d_scores = d_scores[:tok] + d_scores[tok:]
        d_scores = jnp.where(causal, d_scores[:, :tok] + d_scores[:, tok:], 0.0)
        total_ref[:, states] = dot(
            jnp.concatenate(split(d_scores), axis=1), jnp.concatenate([b, b], axis=0)
        )
        gb_ref[:, states] = dot(
            jnp.concatenate(split(d_scores.T), axis=1), jnp.concatenate([c, c], axis=0)
        ).astype(BF16)
        return carry

    lax.fori_loop(0, groups, one_group, 0)

    loads[2].wait()
    loads[3].wait()
    chunk = min(CHUNK, part_width)

    def back_dc(k, s):
        return remote(
            out_dc.at[k, :, pl.ds(s * state_dim, state_dim)],
            got_dc.at[k, :, pl.ds(s * state_dim, state_dim)],
            dc_send.at[k, s],
            dc_recv.at[k, s],
            -k,
        )

    def back_dl(k, s):
        return remote(
            out_dl.at[k, pl.ds(s * part, part), :],
            got_dl.at[k, pl.ds(s * part, part), :],
            dl_send.at[k, s],
            dl_recv.at[k, s],
            -k,
        )

    writes = []
    for s in range(span):

        def one_response(k, carry, s=s):
            @pl.when(k > 0)
            def _():
                if s == 0:
                    send_w(k).wait_recv()
                    send_c(k).wait_recv()
                send_d(k, s).wait_recv()

            c = got_c[k, :, s * state_dim : (s + 1) * state_dim]
            w = got_w[k, s * part : (s + 1) * part, :]
            rows = pl.ds(pl.multiple_of(k * 2 * tok, 2 * tok), 2 * tok)
            d_c = jnp.zeros((2 * tok, state_dim), F32)
            sums = jnp.zeros((part, 2 * tok), F32)
            for start in range(0, part_width, chunk):
                here = slice(s * part_width + start, s * part_width + start + chunk)
                codes = codes_ref[here, :]
                mask = head_mask(part, head_dim, start, chunk)
                v = got_d[k, :, here].astype(F32) * spread(w, mask) * scale_ref[:, here]
                halves = jnp.concatenate(split(v), axis=0)
                parts_ref[rows, start : start + chunk] = halves
                d_c += dot(halves, codes)
                p = v * dot_nt(c, codes)
                sums += dot_nt(mask, jnp.concatenate(split(p), axis=0))
            out_dc[k, :, s * state_dim : (s + 1) * state_dim] = d_c[:tok] + d_c[tok:]
            out_dl[k, s * part : (s + 1) * part, :] = sums[:, :tok] + sums[:, tok:]

            @pl.when(k > 0)
            def _():
                back_dc(k, s).start()
                back_dl(k, s).start()

            flip = c.T
            c_flip[k] = jnp.concatenate([flip, flip], axis=1)
            return carry

        lax.fori_loop(0, count, one_response, 0)

        def one_chunk(j, carry, s=s):
            here = pl.ds(pl.multiple_of(j * chunk, 128), chunk)
            total = jnp.zeros((state_dim, chunk), F32)
            for k in range(count):
                total += dot(c_flip[k], parts_ref[k * 2 * tok : (k + 1) * 2 * tok, here])
            start = pl.multiple_of(s * part_width + j * chunk, 128)
            total = total / scale_ref[:, pl.ds(start, chunk)]
            state_ref[pl.ds(start, chunk), :] = total.T
            return carry

        lax.fori_loop(0, part_width // chunk, one_chunk, 0)
        rows = pl.ds(s * part_width, part_width)
        write = pltpu.make_async_copy(state_ref.at[rows, :], state_hbm.at[rows, :], state_sem.at[s])
        write.start()
        writes.append(write)

    def add_back(owner, d_c, d_l):
        states = state_columns(owner)
        total_ref[:, states] = total_ref[:, states] + d_c
        log_ref[heads_of(owner), :] = d_l

    add_back(me, out_dc[0], out_dl[0])
    for k in range(1, count):
        for s in range(span):
            back_dc(k, s).wait_recv()
            back_dl(k, s).wait_recv()
        add_back(other(k), got_dc[k], got_dl[k])
    gc_ref[...] = total_ref[...].astype(BF16)
    col = col_ref[...]
    d_log = (log_ref[...] + (row_ref[...] - col)).T
    later = dot(jnp.concatenate([upper] * 3, axis=1), three_rows(d_log))
    gdt_ref[...] = (col.T / step - rate * later) / (1.0 + jnp.exp(-dt))

    for k in range(1, count):
        send_w(k).wait_send()
        send_c(k).wait_send()
        for s in range(span):
            send_d(k, s).wait_send()
            back_dc(k, s).wait_send()
            back_dl(k, s).wait_send()
    for write in writes:
        write.wait()


def per_device(
    count,
    inputs,
    cotangent,
    b_proj,
    c_proj,
    dt_raw,
    decay_rate,
    state_codes,
    state_scales,
    sign_bucket,
    adv_scale,
    lengths,
):
    x, d, b, c, dt = inputs[0], cotangent[0], b_proj[0], c_proj[0], dt_raw[0]
    tok, all_heads = dt.shape
    own, head_dim, state_dim = state_codes.shape
    groups = b.shape[1] // state_dim
    span = max(1, own * groups // all_heads)
    part = own // span
    width = own * head_dim
    whole = pl.BlockSpec(memory_space=pltpu.VMEM)
    there = pl.BlockSpec(memory_space=pl.ANY)
    scalar = pl.BlockSpec(memory_space=pltpu.SMEM)
    dma = pltpu.SemaphoreType.DMA
    flops = 24 * tok * tok * x.shape[1] + 12 * count * tok * width * state_dim
    grad_state, grad_b, grad_c, grad_dt = pl.pallas_call(
        functools.partial(kernel, count, groups, head_dim),
        in_specs=[there, there, whole, whole, whole, whole, there, whole, scalar, scalar, scalar],
        out_specs=[there, whole, whole, whole],
        out_shape=[
            jax.ShapeDtypeStruct((width, state_dim), F32),
            jax.ShapeDtypeStruct(b.shape, BF16),
            jax.ShapeDtypeStruct(c.shape, BF16),
            jax.ShapeDtypeStruct(dt.shape, F32),
        ],
        scratch_shapes=[
            pltpu.VMEM(x.shape, BF16),
            pltpu.VMEM(d.shape, BF16),
            pltpu.VMEM((width, state_dim), BF16),
            pltpu.VMEM((width, state_dim), F32),
            pltpu.VMEM((count, tok, width), BF16),
            pltpu.VMEM((count, tok, span * state_dim), BF16),
            pltpu.VMEM((count, own, tok), F32),
            pltpu.VMEM((count * 2 * tok, part * head_dim), BF16),
            pltpu.VMEM((count, state_dim, 2 * tok), BF16),
            pltpu.VMEM((count, tok, span * state_dim), F32),
            pltpu.VMEM((count, own, tok), F32),
            pltpu.VMEM((count, tok, span * state_dim), F32),
            pltpu.VMEM((count, own, tok), F32),
        ]
        + [pltpu.VMEM((all_heads, tok), F32)] * 5
        + [pltpu.VMEM(c.shape, F32), dma((4,)), dma((span,))]
        + [dma((count, span))] * 2
        + [dma((count,))] * 4
        + [dma((count, span))] * 4,
        compiler_params=pltpu.CompilerParams(
            collective_id=0, has_side_effects=True, vmem_limit_bytes=VMEM_BYTES
        ),
        cost_estimate=pl.CostEstimate(
            flops=flops, bytes_accessed=4 * x.size + 8 * width * state_dim, transcendentals=0
        ),
        name="scan_backward",
    )(
        x,
        d,
        b,
        c,
        dt,
        decay_rate.reshape(1, all_heads),
        state_codes.reshape(width, state_dim),
        state_scales.astype(F32).reshape(1, width),
        sign_bucket,
        adv_scale,
        lengths,
    )
    return grad_state.reshape(state_codes.shape), grad_b[None], grad_c[None], grad_dt[None]


def solution(mesh):
    both = ("prompt", "resp")
    return jax.shard_map(
        functools.partial(per_device, mesh.shape["resp"]),
        mesh=mesh,
        in_specs=(
            P(both, None, None),
            P(both, None, None),
            P(both, None, None),
            P(both, None, None),
            P(both, None, None),
            P(),
            P(both, None, None),
            P(both, None),
            P(both),
            P(both),
            P(both),
        ),
        out_specs=(P(both, None, None),) * 4,
        check_vma=False,
    )
```

```python
import functools
import jax
import jax.numpy as jnp
from jax import lax
from jax.experimental import pallas as pl
from jax.experimental.pallas import tpu as pltpu
from jax.sharding import PartitionSpec as P

F32 = jnp.float32
BF16 = jnp.bfloat16
CHUNK = 512
VMEM_BYTES = 56 * 1024 * 1024


def dot(left, right):
    return lax.dot_general(left, right, (((1,), (0,)), ((), ())), preferred_element_type=F32)


def dot_nt(left, right):
    return lax.dot_general(left, right, (((1,), (1,)), ((), ())), preferred_element_type=F32)


def dot_tn(left, right):
    return lax.dot_general(left, right, (((0,), (0,)), ((), ())), preferred_element_type=F32)


def split(value):
    high = value.astype(BF16)
    return high, (value - high.astype(F32)).astype(BF16)


def three_rows(value):
    high = value.astype(BF16)
    middle, low = split(value - high.astype(F32))
    return jnp.concatenate([high, middle, low], axis=0)


def over_rows(weights, head_dim):
    heads, tok = weights.shape
    return jnp.broadcast_to(weights[:, None, :], (heads, head_dim, tok)).reshape(-1, tok)


def head_sums(value, head_dim):
    rows, tok = value.shape
    return jnp.sum(value.reshape(rows // head_dim, head_dim, tok), axis=1)


def kernel(
    count,
    groups,
    head_dim,
    x_hbm,
    d_hbm,
    b_ref,
    c_ref,
    dt_ref,
    rate_ref,
    codes_hbm,
    scale_ref,
    sign_ref,
    adv_ref,
    length_ref,
    state_hbm,
    gb_ref,
    gc_ref,
    gdt_ref,
    x_ref,
    d_ref,
    codes_ref,
    state_ref,
    got_d,
    got_c,
    got_w,
    parts_ref,
    c_twice,
    codes_flip,
    scale_rows,
    out_dc,
    out_dl,
    got_dc,
    got_dl,
    wa_ref,
    wb_ref,
    row_ref,
    col_ref,
    log_ref,
    total_ref,
    load_sem,
    state_sem,
    d_send,
    d_recv,
    c_send,
    c_recv,
    w_send,
    w_recv,
    dc_send,
    dc_recv,
    dl_send,
    dl_recv,
):
    tok, all_heads = dt_ref.shape
    state_dim = b_ref.shape[1] // groups
    group_heads = all_heads // groups
    group_width = group_heads * head_dim
    own = all_heads // count
    width = own * head_dim
    span = max(1, own // group_heads)
    part = own // span
    part_width = part * head_dim
    me = lax.axis_index("resp")

    def other(k):
        return lax.rem(me + k + count, count)

    def first_group(owner):
        return owner * own // group_heads

    barrier = pltpu.get_barrier_semaphore()
    for k in range(1, count):
        pl.semaphore_signal(
            barrier, inc=1, device_id={"resp": other(k)}, device_id_type=pl.DeviceIdType.MESH
        )

    def columns(owner, s):
        return pl.ds(pl.multiple_of(owner * width + s * part_width, 128), part_width)

    loads = [
        pltpu.make_async_copy(x_hbm, x_ref, load_sem.at[0]),
        pltpu.make_async_copy(d_hbm, d_ref, load_sem.at[1]),
        pltpu.make_async_copy(codes_hbm, codes_ref, load_sem.at[2]),
        pltpu.make_async_copy(
            d_hbm.at[:, pl.ds(pl.multiple_of(me * width, 128), width)], got_d.at[0], load_sem.at[3]
        ),
    ]
    for load in loads:
        load.start()
    pl.semaphore_wait(barrier, count - 1)

    def remote(source, target, send, recv, k):
        return pltpu.make_async_remote_copy(
            src_ref=source,
            dst_ref=target,
            send_sem=send,
            recv_sem=recv,
            device_id={"resp": other(k)},
            device_id_type=pl.DeviceIdType.MESH,
        )

    def send_d(k, s):
        return remote(
            d_hbm.at[:, columns(other(k), s)],
            got_d.at[k, :, pl.ds(s * part_width, part_width)],
            d_send.at[k, s],
            d_recv.at[k, s],
            k,
        )

    def state_columns(owner):
        return pl.ds(pl.multiple_of(first_group(owner) * state_dim, 128), span * state_dim)

    def heads_of(owner):
        return pl.ds(pl.multiple_of(owner * own, 8), own)

    def send_c(k):
        return remote(
            c_ref.at[:, state_columns(other(k))], got_c.at[k], c_send.at[k], c_recv.at[k], k
        )

    def send_w(k):
        return remote(wa_ref.at[heads_of(other(k)), :], got_w.at[k], w_send.at[k], w_recv.at[k], k)

    for k in range(1, count):
        send_d(k, 0).start()

    at = lax.broadcasted_iota(jnp.int32, (tok, tok), 0)
    of = lax.broadcasted_iota(jnp.int32, (tok, tok), 1)
    causal = at >= of
    lower = jnp.where(causal, 1.0, 0.0).astype(BF16)
    upper = jnp.where(at <= of, 1.0, 0.0).astype(BF16)
    dt = dt_ref[...]
    step = jnp.maximum(dt, 0.0) + jnp.log1p(jnp.exp(-jnp.abs(dt)))
    rate = rate_ref[...]
    log_decay = -rate * dot(jnp.concatenate([lower] * 3, axis=1), three_rows(step))
    sign = 2.0 * jnp.full((tok, 1), sign_ref[0], jnp.int32).astype(F32) - 1.0
    length = jnp.full((tok, 1), length_ref[0], jnp.int32)
    coefficient = sign * adv_ref[0] / length.astype(F32)
    row_coef = jnp.where(lax.broadcasted_iota(jnp.int32, (tok, 1), 0) < length, coefficient, 0.0)
    wa_ref[...] = (row_coef * jnp.exp(log_decay)).T
    wb_ref[...] = (step * jnp.exp(-log_decay)).T

    for k in range(1, count):
        send_w(k).start()
        send_c(k).start()
    for s in range(1, span):
        for k in range(1, count):
            send_d(k, s).start()
    got_c[0] = c_ref[:, state_columns(me)]
    got_w[0] = wa_ref[heads_of(me), :]
    loads[0].wait()
    loads[1].wait()

    chunk = min(CHUNK, group_width)
    chunk_heads = chunk // head_dim
    nothing = jnp.zeros((tok, tok), BF16)

    def paired(high, low):
        return jnp.concatenate(
            [jnp.concatenate([high, low], axis=1), jnp.concatenate([high, nothing], axis=1)], axis=0
        )

    def one_group(g, carry):
        states = pl.ds(pl.multiple_of(g * state_dim, 128), state_dim)
        b = b_ref[:, states]
        c = c_ref[:, states]
        scores = paired(*split(jnp.where(causal, dot_nt(c, b), 0.0)))
        flipped = paired(*split(jnp.where(at <= of, dot_nt(b, c), 0.0)))
        d_scores = jnp.zeros((2 * tok, 2 * tok), F32)
        for start in range(0, group_width, chunk):
            here = pl.ds(pl.multiple_of(g * group_width + start, 128), chunk)
            heads = pl.ds(
                pl.multiple_of(g * group_heads + start // head_dim, chunk_heads), chunk_heads
            )
            w = d_ref[:, here].T.astype(F32) * over_rows(wa_ref[heads, :], head_dim)
            x = x_ref[:, here].T.astype(F32) * over_rows(wb_ref[heads, :], head_dim)
            w_parts = jnp.concatenate(split(w), axis=1)
            x_parts = jnp.concatenate(split(x), axis=1)
            d_scores += dot_tn(w_parts, x_parts)
            y = dot(x_parts, flipped)
            u = dot(w_parts, scores)
            row_ref[heads, :] = head_sums(w * (y[:, :tok] + y[:, tok:]), head_dim)
            col_ref[heads, :] = head_sums(x * (u[:, :tok] + u[:, tok:]), head_dim)
        d_scores = d_scores[:tok] + d_scores[tok:]
        d_scores = jnp.where(causal, d_scores[:, :tok] + d_scores[:, tok:], 0.0)
        total_ref[:, states] = dot(
            jnp.concatenate(split(d_scores), axis=1), jnp.concatenate([b, b], axis=0)
        )
        gb_ref[:, states] = dot(
            jnp.concatenate(split(d_scores.T), axis=1), jnp.concatenate([c, c], axis=0)
        ).astype(BF16)
        return carry

    lax.fori_loop(0, groups, one_group, 0)

    loads[2].wait()
    loads[3].wait()
    chunk = min(CHUNK, part_width)
    chunk_heads = chunk // head_dim
    scales = scale_ref[...].astype(F32).T
    for h in range(own):
        scale_rows[h * head_dim : (h + 1) * head_dim, :] = jnp.broadcast_to(
            scales[:, h : h + 1], (head_dim, tok)
        )
    for start in range(0, width, chunk):
        codes_flip[:, start : start + chunk] = codes_ref[start : start + chunk, :].T

    def back_dc(k, s):
        return remote(
            out_dc.at[k, :, pl.ds(s * state_dim, state_dim)],
            got_dc.at[k, :, pl.ds(s * state_dim, state_dim)],
            dc_send.at[k, s],
            dc_recv.at[k, s],
            -k,
        )

    def back_dl(k, s):
        return remote(
            out_dl.at[k, pl.ds(s * part, part), :],
            got_dl.at[k, pl.ds(s * part, part), :],
            dl_send.at[k, s],
            dl_recv.at[k, s],
            -k,
        )

    writes = []
    for s in range(span):

        def one_response(k, carry, s=s):
            @pl.when(k > 0)
            def _():
                if s == 0:
                    send_w(k).wait_recv()
                    send_c(k).wait_recv()
                send_d(k, s).wait_recv()

            lanes = pl.ds(pl.multiple_of(k * 2 * tok, 128), 2 * tok)
            c = got_c[k, :, s * state_dim : (s + 1) * state_dim]
            c_flip = c.T
            d_c = jnp.zeros((state_dim, 2 * tok), F32)
            for start in range(0, part_width, chunk):
                here = slice(s * part_width + start, s * part_width + start + chunk)
                first = s * part + start // head_dim
                heads = slice(first, first + chunk_heads)
                v = got_d[k, :, here].T.astype(F32) * over_rows(got_w[k, heads, :], head_dim)
                v = v * scale_rows[here, :]
                v_parts = jnp.concatenate(split(v), axis=1)
                parts_ref[start : start + chunk, lanes] = v_parts
                d_c += dot(codes_flip[:, here], v_parts)
                out_dl[k, heads, :] = head_sums(v * dot(codes_ref[here, :], c_flip), head_dim)
            out_dc[k, :, s * state_dim : (s + 1) * state_dim] = (d_c[:, :tok] + d_c[:, tok:]).T

            @pl.when(k > 0)
            def _():
                back_dc(k, s).start()
                back_dl(k, s).start()

            c_twice[lanes, :] = jnp.concatenate([c, c], axis=0)
            return carry

        lax.fori_loop(0, count, one_response, 0)

        def one_chunk(j, carry, s=s):
            rows = pl.ds(pl.multiple_of(j * chunk, chunk), chunk)
            here = pl.ds(pl.multiple_of(s * part_width + j * chunk, chunk), chunk)
            inverse = 1.0 / scale_rows[here, :]
            wide = jnp.concatenate([inverse] * (state_dim // tok), axis=1)
            state_ref[here, :] = dot(parts_ref[rows, :], c_twice[...]) * wide
            return carry

        lax.fori_loop(0, part_width // chunk, one_chunk, 0)
        rows = pl.ds(s * part_width, part_width)
        write = pltpu.make_async_copy(state_ref.at[rows, :], state_hbm.at[rows, :], state_sem.at[s])
        write.start()
        writes.append(write)

    def add_back(owner, d_c, d_l):
        states = state_columns(owner)
        total_ref[:, states] = total_ref[:, states] + d_c
        log_ref[heads_of(owner), :] = d_l

    add_back(me, out_dc[0], out_dl[0])
    for k in range(1, count):
        for s in range(span):
            back_dc(k, s).wait_recv()
            back_dl(k, s).wait_recv()
        add_back(other(k), got_dc[k], got_dl[k])
    gc_ref[...] = total_ref[...].astype(BF16)
    col = col_ref[...]
    d_log = (log_ref[...] + (row_ref[...] - col)).T
    later = dot(jnp.concatenate([upper] * 3, axis=1), three_rows(d_log))
    gdt_ref[...] = (col.T / step - rate * later) / (1.0 + jnp.exp(-dt))

    for k in range(1, count):
        send_w(k).wait_send()
        send_c(k).wait_send()
        for s in range(span):
            send_d(k, s).wait_send()
            back_dc(k, s).wait_send()
            back_dl(k, s).wait_send()
    for write in writes:
        write.wait()


def per_device(
    count,
    inputs,
    cotangent,
    b_proj,
    c_proj,
    dt_raw,
    decay_rate,
    state_codes,
    state_scales,
    sign_bucket,
    adv_scale,
    lengths,
):
    x, d, b, c, dt = inputs[0], cotangent[0], b_proj[0], c_proj[0], dt_raw[0]
    tok, all_heads = dt.shape
    own, head_dim, state_dim = state_codes.shape
    groups = b.shape[1] // state_dim
    span = max(1, own * groups // all_heads)
    part = own // span
    width = own * head_dim
    whole = pl.BlockSpec(memory_space=pltpu.VMEM)
    there = pl.BlockSpec(memory_space=pl.ANY)
    scalar = pl.BlockSpec(memory_space=pltpu.SMEM)
    dma = pltpu.SemaphoreType.DMA
    flops = 24 * tok * tok * x.shape[1] + 12 * count * tok * width * state_dim
    grad_state, grad_b, grad_c, grad_dt = pl.pallas_call(
        functools.partial(kernel, count, groups, head_dim),
        in_specs=[there, there, whole, whole, whole, whole, there, whole, scalar, scalar, scalar],
        out_specs=[there, whole, whole, whole],
        out_shape=[
            jax.ShapeDtypeStruct((width, state_dim), F32),
            jax.ShapeDtypeStruct(b.shape, BF16),
            jax.ShapeDtypeStruct(c.shape, BF16),
            jax.ShapeDtypeStruct(dt.shape, F32),
        ],
        scratch_shapes=[
            pltpu.VMEM(x.shape, BF16),
            pltpu.VMEM(d.shape, BF16),
            pltpu.VMEM((width, state_dim), BF16),
            pltpu.VMEM((width, state_dim), F32),
            pltpu.VMEM((count, tok, width), BF16),
            pltpu.VMEM((count, tok, span * state_dim), BF16),
            pltpu.VMEM((count, own, tok), F32),
            pltpu.VMEM((part * head_dim, count * 2 * tok), BF16),
            pltpu.VMEM((count * 2 * tok, state_dim), BF16),
            pltpu.VMEM((state_dim, width), BF16),
            pltpu.VMEM((width, tok), F32),
            pltpu.VMEM((count, tok, span * state_dim), F32),
            pltpu.VMEM((count, own, tok), F32),
            pltpu.VMEM((count, tok, span * state_dim), F32),
            pltpu.VMEM((count, own, tok), F32),
        ]
        + [pltpu.VMEM((all_heads, tok), F32)] * 5
        + [pltpu.VMEM(c.shape, F32), dma((4,)), dma((span,))]
        + [dma((count, span))] * 2
        + [dma((count,))] * 4
        + [dma((count, span))] * 4,
        compiler_params=pltpu.CompilerParams(
            collective_id=0, has_side_effects=True, vmem_limit_bytes=VMEM_BYTES
        ),
        cost_estimate=pl.CostEstimate(
            flops=flops, bytes_accessed=4 * x.size + 8 * width * state_dim, transcendentals=0
        ),
        name="scan_backward",
    )(
        x,
        d,
        b,
        c,
        dt,
        decay_rate.reshape(1, all_heads),
        state_codes.reshape(width, state_dim),
        state_scales,
        sign_bucket,
        adv_scale,
        lengths,
    )
    return grad_state.reshape(state_codes.shape), grad_b[None], grad_c[None], grad_dt[None]


def solution(mesh):
    both = ("prompt", "resp")
    return jax.shard_map(
        functools.partial(per_device, mesh.shape["resp"]),
        mesh=mesh,
        in_specs=(
            P(both, None, None),
            P(both, None, None),
            P(both, None, None),
            P(both, None, None),
            P(both, None, None),
            P(),
            P(both, None, None),
            P(both, None),
            P(both),
            P(both),
            P(both),
        ),
        out_specs=(P(both, None, None),) * 4,
        check_vma=False,
    )
```

```python
import functools
import jax
import jax.numpy as jnp
from jax import lax
from jax.experimental import pallas as pl
from jax.experimental.pallas import tpu as pltpu
from jax.sharding import PartitionSpec as P

F32 = jnp.float32
BF16 = jnp.bfloat16
CHUNK = 512
VMEM_BYTES = 56 * 1024 * 1024


def dot(left, right):
    return lax.dot_general(left, right, (((1,), (0,)), ((), ())), preferred_element_type=F32)


def dot_nt(left, right):
    return lax.dot_general(left, right, (((1,), (1,)), ((), ())), preferred_element_type=F32)


def dot_tn(left, right):
    return lax.dot_general(left, right, (((0,), (0,)), ((), ())), preferred_element_type=F32)


def split(value):
    high = value.astype(BF16)
    return high, (value - high.astype(F32)).astype(BF16)


def three_rows(value):
    high = value.astype(BF16)
    middle, low = split(value - high.astype(F32))
    return jnp.concatenate([high, middle, low], axis=0)


def over_rows(weights, head_dim):
    heads, tok = weights.shape
    return jnp.broadcast_to(weights[:, None, :], (heads, head_dim, tok)).reshape(-1, tok)


def head_sums(value, head_dim):
    rows, tok = value.shape
    return jnp.sum(value.reshape(rows // head_dim, head_dim, tok), axis=1)


def kernel(
    count,
    groups,
    head_dim,
    x_hbm,
    d_hbm,
    b_ref,
    c_ref,
    dt_ref,
    rate_ref,
    codes_hbm,
    scale_ref,
    sign_ref,
    adv_ref,
    length_ref,
    state_hbm,
    gb_ref,
    gc_ref,
    gdt_ref,
    x_ref,
    d_ref,
    codes_ref,
    state_ref,
    got_d,
    got_c,
    got_w,
    parts_ref,
    c_twice,
    codes_flip,
    scale_rows,
    out_dc,
    out_dl,
    got_dc,
    got_dl,
    wa_ref,
    wb_ref,
    row_ref,
    col_ref,
    log_ref,
    total_ref,
    load_sem,
    state_sem,
    d_send,
    d_recv,
    c_send,
    c_recv,
    w_send,
    w_recv,
    dc_send,
    dc_recv,
    dl_send,
    dl_recv,
):
    tok, all_heads = dt_ref.shape
    state_dim = b_ref.shape[1] // groups
    group_heads = all_heads // groups
    group_width = group_heads * head_dim
    own = all_heads // count
    width = own * head_dim
    span = max(1, own // group_heads)
    part = own // span
    part_width = part * head_dim
    me = lax.axis_index("resp")

    def other(k):
        return lax.rem(me + k + count, count)

    def first_group(owner):
        return owner * own // group_heads

    barrier = pltpu.get_barrier_semaphore()
    for k in range(1, count):
        pl.semaphore_signal(
            barrier, inc=1, device_id={"resp": other(k)}, device_id_type=pl.DeviceIdType.MESH
        )

    def columns(owner, s):
        return pl.ds(pl.multiple_of(owner * width + s * part_width, 128), part_width)

    loads = [
        pltpu.make_async_copy(x_hbm, x_ref, load_sem.at[0]),
        pltpu.make_async_copy(d_hbm, d_ref, load_sem.at[1]),
        pltpu.make_async_copy(codes_hbm, codes_ref, load_sem.at[2]),
        pltpu.make_async_copy(
            d_hbm.at[:, pl.ds(pl.multiple_of(me * width, 128), width)], got_d.at[0], load_sem.at[3]
        ),
    ]
    for load in loads:
        load.start()
    pl.semaphore_wait(barrier, count - 1)

    def remote(source, target, send, recv, k):
        return pltpu.make_async_remote_copy(
            src_ref=source,
            dst_ref=target,
            send_sem=send,
            recv_sem=recv,
            device_id={"resp": other(k)},
            device_id_type=pl.DeviceIdType.MESH,
        )

    def send_d(k, s):
        return remote(
            d_hbm.at[:, columns(other(k), s)],
            got_d.at[k, :, pl.ds(s * part_width, part_width)],
            d_send.at[k, s],
            d_recv.at[k, s],
            k,
        )

    def state_columns(owner):
        return pl.ds(pl.multiple_of(first_group(owner) * state_dim, 128), span * state_dim)

    def heads_of(owner):
        return pl.ds(pl.multiple_of(owner * own, 8), own)

    def send_c(k):
        return remote(
            c_ref.at[:, state_columns(other(k))], got_c.at[k], c_send.at[k], c_recv.at[k], k
        )

    def send_w(k):
        return remote(wa_ref.at[heads_of(other(k)), :], got_w.at[k], w_send.at[k], w_recv.at[k], k)

    for k in range(1, count):
        send_d(k, 0).start()

    at = lax.broadcasted_iota(jnp.int32, (tok, tok), 0)
    of = lax.broadcasted_iota(jnp.int32, (tok, tok), 1)
    causal = at >= of
    lower = jnp.where(causal, 1.0, 0.0).astype(BF16)
    upper = jnp.where(at <= of, 1.0, 0.0).astype(BF16)
    dt = dt_ref[...]
    step = jnp.maximum(dt, 0.0) + jnp.log1p(jnp.exp(-jnp.abs(dt)))
    rate = rate_ref[...]
    log_decay = -rate * dot(jnp.concatenate([lower] * 3, axis=1), three_rows(step))
    sign = 2.0 * jnp.full((tok, 1), sign_ref[0], jnp.int32).astype(F32) - 1.0
    length = jnp.full((tok, 1), length_ref[0], jnp.int32)
    coefficient = sign * adv_ref[0] / length.astype(F32)
    row_coef = jnp.where(lax.broadcasted_iota(jnp.int32, (tok, 1), 0) < length, coefficient, 0.0)
    wa_ref[...] = (row_coef * jnp.exp(log_decay)).T
    wb_ref[...] = (step * jnp.exp(-log_decay)).T

    for k in range(1, count):
        send_w(k).start()
        send_c(k).start()
    for s in range(1, span):
        for k in range(1, count):
            send_d(k, s).start()
    got_c[0] = c_ref[:, state_columns(me)]
    got_w[0] = wa_ref[heads_of(me), :]
    loads[0].wait()
    loads[1].wait()

    chunk = min(CHUNK, group_width)
    chunk_heads = chunk // head_dim
    nothing = jnp.zeros((tok, tok), BF16)

    def paired(high, low):
        return jnp.concatenate(
            [jnp.concatenate([high, low], axis=1), jnp.concatenate([high, nothing], axis=1)], axis=0
        )

    def one_group(g, carry):
        states = pl.ds(pl.multiple_of(g * state_dim, 128), state_dim)
        b = b_ref[:, states]
        c = c_ref[:, states]
        scores = paired(*split(jnp.where(causal, dot_nt(c, b), 0.0)))
        flipped = paired(*split(jnp.where(at <= of, dot_nt(b, c), 0.0)))
        d_scores = jnp.zeros((2 * tok, 2 * tok), F32)
        for start in range(0, group_width, chunk):
            here = pl.ds(pl.multiple_of(g * group_width + start, 128), chunk)
            heads = pl.ds(
                pl.multiple_of(g * group_heads + start // head_dim, chunk_heads), chunk_heads
            )
            w = d_ref[:, here].T.astype(F32) * over_rows(wa_ref[heads, :], head_dim)
            x = x_ref[:, here].T.astype(F32) * over_rows(wb_ref[heads, :], head_dim)
            w_parts = jnp.concatenate(split(w), axis=1)
            x_parts = jnp.concatenate(split(x), axis=1)
            d_scores += dot_tn(w_parts, x_parts)
            y = dot(x_parts, flipped)
            u = dot(w_parts, scores)
            row_ref[heads, :] = head_sums(w * (y[:, :tok] + y[:, tok:]), head_dim)
            col_ref[heads, :] = head_sums(x * (u[:, :tok] + u[:, tok:]), head_dim)
        d_scores = d_scores[:tok] + d_scores[tok:]
        d_scores = jnp.where(causal, d_scores[:, :tok] + d_scores[:, tok:], 0.0)
        total_ref[:, states] = dot(
            jnp.concatenate(split(d_scores), axis=1), jnp.concatenate([b, b], axis=0)
        )
        gb_ref[:, states] = dot(
            jnp.concatenate(split(d_scores.T), axis=1), jnp.concatenate([c, c], axis=0)
        ).astype(BF16)
        return carry

    lax.fori_loop(0, groups, one_group, 0)

    loads[2].wait()
    loads[3].wait()
    chunk = min(CHUNK, part_width)
    chunk_heads = chunk // head_dim
    scales = scale_ref[...].astype(F32).T
    for h in range(own):
        scale_rows[h * head_dim : (h + 1) * head_dim, :] = jnp.broadcast_to(
            scales[:, h : h + 1], (head_dim, tok)
        )
    for start in range(0, width, chunk):
        codes_flip[:, start : start + chunk] = codes_ref[start : start + chunk, :].T

    def back_dc(k, s):
        return remote(
            out_dc.at[k, :, pl.ds(s * state_dim, state_dim)],
            got_dc.at[k, :, pl.ds(s * state_dim, state_dim)],
            dc_send.at[k, s],
            dc_recv.at[k, s],
            -k,
        )

    def back_dl(k, s):
        return remote(
            out_dl.at[k, pl.ds(s * part, part), :],
            got_dl.at[k, pl.ds(s * part, part), :],
            dl_send.at[k, s],
            dl_recv.at[k, s],
            -k,
        )

    writes = []
    for s in range(span):

        def one_response(k, carry, s=s):
            @pl.when(k > 0)
            def _():
                if s == 0:
                    send_w(k).wait_recv()
                    send_c(k).wait_recv()
                send_d(k, s).wait_recv()

            lanes = pl.ds(pl.multiple_of(k * 2 * tok, 128), 2 * tok)
            c = got_c[k, :, s * state_dim : (s + 1) * state_dim]
            c_flip = c.T
            d_c = jnp.zeros((state_dim, 2 * tok), F32)
            for start in range(0, part_width, chunk):
                here = slice(s * part_width + start, s * part_width + start + chunk)
                first = s * part + start // head_dim
                heads = slice(first, first + chunk_heads)
                v = got_d[k, :, here].T.astype(F32) * over_rows(got_w[k, heads, :], head_dim)
                v = v * scale_rows[here, :]
                v_parts = jnp.concatenate(split(v), axis=1)
                parts_ref[start : start + chunk, lanes] = v_parts
                d_c += dot(codes_flip[:, here], v_parts)
                out_dl[k, heads, :] = head_sums(v * dot(codes_ref[here, :], c_flip), head_dim)
            out_dc[k, :, s * state_dim : (s + 1) * state_dim] = (d_c[:, :tok] + d_c[:, tok:]).T

            @pl.when(k > 0)
            def _():
                back_dc(k, s).start()
                back_dl(k, s).start()

            c_twice[lanes, :] = jnp.concatenate([c, c], axis=0)
            return carry

        lax.fori_loop(0, count, one_response, 0)

        def one_chunk(j, carry, s=s):
            rows = pl.ds(pl.multiple_of(j * chunk, chunk), chunk)
            here = pl.ds(pl.multiple_of(s * part_width + j * chunk, chunk), chunk)
            inverse = 1.0 / scale_rows[here, :]
            wide = jnp.concatenate([inverse] * (state_dim // tok), axis=1)
            state_ref[here, :] = dot(parts_ref[rows, :], c_twice[...]) * wide
            return carry

        lax.fori_loop(0, part_width // chunk, one_chunk, 0)
        rows = pl.ds(s * part_width, part_width)
        write = pltpu.make_async_copy(state_ref.at[rows, :], state_hbm.at[rows, :], state_sem.at[s])
        write.start()
        writes.append(write)

    def add_back(owner, d_c, d_l):
        states = state_columns(owner)
        total_ref[:, states] = total_ref[:, states] + d_c
        log_ref[heads_of(owner), :] = d_l

    add_back(me, out_dc[0], out_dl[0])
    for k in range(1, count):
        for s in range(span):
            back_dc(k, s).wait_recv()
            back_dl(k, s).wait_recv()
        add_back(other(k), got_dc[k], got_dl[k])
    gc_ref[...] = total_ref[...].astype(BF16)
    col = col_ref[...]
    d_log = (log_ref[...] + (row_ref[...] - col)).T
    later = dot(jnp.concatenate([upper] * 3, axis=1), three_rows(d_log))
    gdt_ref[...] = (col.T / step - rate * later) / (1.0 + jnp.exp(-dt))

    for k in range(1, count):
        send_w(k).wait_send()
        send_c(k).wait_send()
        for s in range(span):
            send_d(k, s).wait_send()
            back_dc(k, s).wait_send()
            back_dl(k, s).wait_send()
    for write in writes:
        write.wait()


PIECES = 8


def copy_kernel(state_from, gb_from, gc_from, gdt_from, state_to, gb_to, gc_to, gdt_to, sem):
    rows = state_from.shape[0] // PIECES
    copies = [
        pltpu.make_async_copy(
            state_from.at[pl.ds(i * rows, rows), :], state_to.at[pl.ds(i * rows, rows), :], sem.at[i]
        )
        for i in range(PIECES)
    ]
    small = ((gb_from, gb_to), (gc_from, gc_to), (gdt_from, gdt_to))
    for i, (source, target) in enumerate(small):
        copies.append(pltpu.make_async_copy(source, target, sem.at[PIECES + i]))
    for copy in copies:
        copy.start()
    for copy in copies:
        copy.wait()


def copied(*results):
    there = pl.BlockSpec(memory_space=pl.ANY)
    return pl.pallas_call(
        copy_kernel,
        in_specs=[there] * 4,
        out_specs=[there] * 4,
        out_shape=[jax.ShapeDtypeStruct(result.shape, result.dtype) for result in results],
        scratch_shapes=[pltpu.SemaphoreType.DMA((PIECES + 3,))],
        compiler_params=pltpu.CompilerParams(vmem_limit_bytes=VMEM_BYTES),
        name="copy_results",
    )(*results)


def per_device(
    count,
    inputs,
    cotangent,
    b_proj,
    c_proj,
    dt_raw,
    decay_rate,
    state_codes,
    state_scales,
    sign_bucket,
    adv_scale,
    lengths,
):
    x, d, b, c, dt = inputs[0], cotangent[0], b_proj[0], c_proj[0], dt_raw[0]
    tok, all_heads = dt.shape
    own, head_dim, state_dim = state_codes.shape
    groups = b.shape[1] // state_dim
    span = max(1, own * groups // all_heads)
    part = own // span
    width = own * head_dim
    whole = pl.BlockSpec(memory_space=pltpu.VMEM)
    there = pl.BlockSpec(memory_space=pl.ANY)
    scalar = pl.BlockSpec(memory_space=pltpu.SMEM)
    dma = pltpu.SemaphoreType.DMA
    flops = 24 * tok * tok * x.shape[1] + 12 * count * tok * width * state_dim
    results = pl.pallas_call(
        functools.partial(kernel, count, groups, head_dim),
        in_specs=[there, there, whole, whole, whole, whole, there, whole, scalar, scalar, scalar],
        out_specs=[there, whole, whole, whole],
        out_shape=[
            jax.ShapeDtypeStruct((width, state_dim), F32),
            jax.ShapeDtypeStruct(b.shape, BF16),
            jax.ShapeDtypeStruct(c.shape, BF16),
            jax.ShapeDtypeStruct(dt.shape, F32),
        ],
        scratch_shapes=[
            pltpu.VMEM(x.shape, BF16),
            pltpu.VMEM(d.shape, BF16),
            pltpu.VMEM((width, state_dim), BF16),
            pltpu.VMEM((width, state_dim), F32),
            pltpu.VMEM((count, tok, width), BF16),
            pltpu.VMEM((count, tok, span * state_dim), BF16),
            pltpu.VMEM((count, own, tok), F32),
            pltpu.VMEM((part * head_dim, count * 2 * tok), BF16),
            pltpu.VMEM((count * 2 * tok, state_dim), BF16),
            pltpu.VMEM((state_dim, width), BF16),
            pltpu.VMEM((width, tok), F32),
            pltpu.VMEM((count, tok, span * state_dim), F32),
            pltpu.VMEM((count, own, tok), F32),
            pltpu.VMEM((count, tok, span * state_dim), F32),
            pltpu.VMEM((count, own, tok), F32),
        ]
        + [pltpu.VMEM((all_heads, tok), F32)] * 5
        + [pltpu.VMEM(c.shape, F32), dma((4,)), dma((span,))]
        + [dma((count, span))] * 2
        + [dma((count,))] * 4
        + [dma((count, span))] * 4,
        compiler_params=pltpu.CompilerParams(
            collective_id=0, has_side_effects=True, vmem_limit_bytes=VMEM_BYTES
        ),
        cost_estimate=pl.CostEstimate(
            flops=flops, bytes_accessed=4 * x.size + 8 * width * state_dim, transcendentals=0
        ),
        name="scan_backward",
    )(
        x,
        d,
        b,
        c,
        dt,
        decay_rate.reshape(1, all_heads),
        state_codes.reshape(width, state_dim),
        state_scales,
        sign_bucket,
        adv_scale,
        lengths,
    )
    grad_state, grad_b, grad_c, grad_dt = copied(*results)
    return grad_state.reshape(state_codes.shape), grad_b[None], grad_c[None], grad_dt[None]


def solution(mesh):
    both = ("prompt", "resp")
    return jax.shard_map(
        functools.partial(per_device, mesh.shape["resp"]),
        mesh=mesh,
        in_specs=(
            P(both, None, None),
            P(both, None, None),
            P(both, None, None),
            P(both, None, None),
            P(both, None, None),
            P(),
            P(both, None, None),
            P(both, None),
            P(both),
            P(both),
            P(both),
        ),
        out_specs=(P(both, None, None),) * 4,
        check_vma=False,
    )
```

```python
import functools
import jax
import jax.numpy as jnp
from jax import lax
from jax.experimental import pallas as pl
from jax.experimental.pallas import tpu as pltpu
from jax.sharding import PartitionSpec as P

F32 = jnp.float32
BF16 = jnp.bfloat16
CHUNK = 512
VMEM_BYTES = 56 * 1024 * 1024


def dot(left, right):
    return lax.dot_general(left, right, (((1,), (0,)), ((), ())), preferred_element_type=F32)


def dot_nt(left, right):
    return lax.dot_general(left, right, (((1,), (1,)), ((), ())), preferred_element_type=F32)


def dot_tn(left, right):
    return lax.dot_general(left, right, (((0,), (0,)), ((), ())), preferred_element_type=F32)


def split(value):
    high = value.astype(BF16)
    return high, (value - high.astype(F32)).astype(BF16)


def three_rows(value):
    high = value.astype(BF16)
    middle, low = split(value - high.astype(F32))
    return jnp.concatenate([high, middle, low], axis=0)


def over_rows(weights, head_dim):
    heads, tok = weights.shape
    return jnp.broadcast_to(weights[:, None, :], (heads, head_dim, tok)).reshape(-1, tok)


def head_sums(value, head_dim):
    rows, tok = value.shape
    return jnp.sum(value.reshape(rows // head_dim, head_dim, tok), axis=1)


def kernel(
    count,
    groups,
    head_dim,
    x_hbm,
    d_hbm,
    b_ref,
    c_ref,
    dt_ref,
    rate_ref,
    codes_hbm,
    scale_ref,
    sign_ref,
    adv_ref,
    length_ref,
    state_hbm,
    gb_ref,
    gc_ref,
    gdt_ref,
    x_ref,
    d_ref,
    codes_ref,
    state_ref,
    got_d,
    got_c,
    got_w,
    parts_ref,
    c_twice,
    codes_flip,
    scale_rows,
    out_dc,
    out_dl,
    got_dc,
    got_dl,
    wa_ref,
    wb_ref,
    row_ref,
    col_ref,
    log_ref,
    total_ref,
    load_sem,
    state_sem,
    d_send,
    d_recv,
    c_send,
    c_recv,
    w_send,
    w_recv,
    dc_send,
    dc_recv,
    dl_send,
    dl_recv,
):
    tok, all_heads = dt_ref.shape
    state_dim = b_ref.shape[1] // groups
    group_heads = all_heads // groups
    group_width = group_heads * head_dim
    own = all_heads // count
    width = own * head_dim
    span = max(1, own // group_heads)
    part = own // span
    part_width = part * head_dim
    me = lax.axis_index("resp")

    def other(k):
        return lax.rem(me + k + count, count)

    def first_group(owner):
        return owner * own // group_heads

    barrier = pltpu.get_barrier_semaphore()
    for k in range(1, count):
        pl.semaphore_signal(
            barrier, inc=1, device_id={"resp": other(k)}, device_id_type=pl.DeviceIdType.MESH
        )

    def columns(owner, s):
        return pl.ds(pl.multiple_of(owner * width + s * part_width, 128), part_width)

    loads = [
        pltpu.make_async_copy(x_hbm, x_ref, load_sem.at[0]),
        pltpu.make_async_copy(d_hbm, d_ref, load_sem.at[1]),
        pltpu.make_async_copy(codes_hbm, codes_ref, load_sem.at[2]),
        pltpu.make_async_copy(
            d_hbm.at[:, pl.ds(pl.multiple_of(me * width, 128), width)], got_d.at[0], load_sem.at[3]
        ),
    ]
    for load in loads:
        load.start()
    pl.semaphore_wait(barrier, count - 1)

    def remote(source, target, send, recv, k):
        return pltpu.make_async_remote_copy(
            src_ref=source,
            dst_ref=target,
            send_sem=send,
            recv_sem=recv,
            device_id={"resp": other(k)},
            device_id_type=pl.DeviceIdType.MESH,
        )

    def send_d(k, s):
        return remote(
            d_hbm.at[:, columns(other(k), s)],
            got_d.at[k, :, pl.ds(s * part_width, part_width)],
            d_send.at[k, s],
            d_recv.at[k, s],
            k,
        )

    def state_columns(owner):
        return pl.ds(pl.multiple_of(first_group(owner) * state_dim, 128), span * state_dim)

    def heads_of(owner):
        return pl.ds(pl.multiple_of(owner * own, 8), own)

    def send_c(k):
        return remote(
            c_ref.at[:, state_columns(other(k))], got_c.at[k], c_send.at[k], c_recv.at[k], k
        )

    def send_w(k):
        return remote(wa_ref.at[heads_of(other(k)), :], got_w.at[k], w_send.at[k], w_recv.at[k], k)

    for k in range(1, count):
        send_d(k, 0).start()

    at = lax.broadcasted_iota(jnp.int32, (tok, tok), 0)
    of = lax.broadcasted_iota(jnp.int32, (tok, tok), 1)
    causal = at >= of
    lower = jnp.where(causal, 1.0, 0.0).astype(BF16)
    upper = jnp.where(at <= of, 1.0, 0.0).astype(BF16)
    dt = dt_ref[...]
    step = jnp.maximum(dt, 0.0) + jnp.log1p(jnp.exp(-jnp.abs(dt)))
    rate = rate_ref[...]
    log_decay = -rate * dot(jnp.concatenate([lower] * 3, axis=1), three_rows(step))
    sign = 2.0 * jnp.full((tok, 1), sign_ref[0], jnp.int32).astype(F32) - 1.0
    length = jnp.full((tok, 1), length_ref[0], jnp.int32)
    coefficient = sign * adv_ref[0] / length.astype(F32)
    row_coef = jnp.where(lax.broadcasted_iota(jnp.int32, (tok, 1), 0) < length, coefficient, 0.0)
    wa_ref[...] = (row_coef * jnp.exp(log_decay)).T
    wb_ref[...] = (step * jnp.exp(-log_decay)).T

    for k in range(1, count):
        send_w(k).start()
        send_c(k).start()
    for s in range(1, span):
        for k in range(1, count):
            send_d(k, s).start()
    got_c[0] = c_ref[:, state_columns(me)]
    got_w[0] = wa_ref[heads_of(me), :]
    loads[0].wait()
    loads[1].wait()

    chunk = min(CHUNK, group_width)
    chunk_heads = chunk // head_dim
    nothing = jnp.zeros((tok, tok), BF16)

    def paired(high, low):
        return jnp.concatenate(
            [jnp.concatenate([high, low], axis=1), jnp.concatenate([high, nothing], axis=1)], axis=0
        )

    def one_group(g, carry):
        states = pl.ds(pl.multiple_of(g * state_dim, 128), state_dim)
        b = b_ref[:, states]
        c = c_ref[:, states]
        scores = paired(*split(jnp.where(causal, dot_nt(c, b), 0.0)))
        flipped = paired(*split(jnp.where(at <= of, dot_nt(b, c), 0.0)))
        d_scores = jnp.zeros((2 * tok, 2 * tok), F32)
        for start in range(0, group_width, chunk):
            here = pl.ds(pl.multiple_of(g * group_width + start, 128), chunk)
            heads = pl.ds(
                pl.multiple_of(g * group_heads + start // head_dim, chunk_heads), chunk_heads
            )
            w = d_ref[:, here].T.astype(F32) * over_rows(wa_ref[heads, :], head_dim)
            x = x_ref[:, here].T.astype(F32) * over_rows(wb_ref[heads, :], head_dim)
            w_parts = jnp.concatenate(split(w), axis=1)
            x_parts = jnp.concatenate(split(x), axis=1)
            d_scores += dot_tn(w_parts, x_parts)
            y = dot(x_parts, flipped)
            u = dot(w_parts, scores)
            row_ref[heads, :] = head_sums(w * (y[:, :tok] + y[:, tok:]), head_dim)
            col_ref[heads, :] = head_sums(x * (u[:, :tok] + u[:, tok:]), head_dim)
        d_scores = d_scores[:tok] + d_scores[tok:]
        d_scores = jnp.where(causal, d_scores[:, :tok] + d_scores[:, tok:], 0.0)
        total_ref[:, states] = dot(
            jnp.concatenate(split(d_scores), axis=1), jnp.concatenate([b, b], axis=0)
        )
        gb_ref[:, states] = dot(
            jnp.concatenate(split(d_scores.T), axis=1), jnp.concatenate([c, c], axis=0)
        ).astype(BF16)
        return carry

    lax.fori_loop(0, groups, one_group, 0)

    loads[2].wait()
    loads[3].wait()
    chunk = min(CHUNK, part_width)
    chunk_heads = chunk // head_dim
    scales = scale_ref[...].astype(F32).T
    for h in range(own):
        scale_rows[h * head_dim : (h + 1) * head_dim, :] = jnp.broadcast_to(
            scales[:, h : h + 1], (head_dim, tok)
        )
    for start in range(0, width, chunk):
        codes_flip[:, start : start + chunk] = codes_ref[start : start + chunk, :].T

    def back_dc(k, s):
        return remote(
            out_dc.at[k, :, pl.ds(s * state_dim, state_dim)],
            got_dc.at[k, :, pl.ds(s * state_dim, state_dim)],
            dc_send.at[k, s],
            dc_recv.at[k, s],
            -k,
        )

    def back_dl(k, s):
        return remote(
            out_dl.at[k, pl.ds(s * part, part), :],
            got_dl.at[k, pl.ds(s * part, part), :],
            dl_send.at[k, s],
            dl_recv.at[k, s],
            -k,
        )

    writes = []
    for s in range(span):

        def one_response(k, carry, s=s):
            @pl.when(k > 0)
            def _():
                if s == 0:
                    send_w(k).wait_recv()
                    send_c(k).wait_recv()
                send_d(k, s).wait_recv()

            lanes = pl.ds(pl.multiple_of(k * 2 * tok, 128), 2 * tok)
            c = got_c[k, :, s * state_dim : (s + 1) * state_dim]
            c_flip = c.T
            d_c = jnp.zeros((state_dim, 2 * tok), F32)
            for start in range(0, part_width, chunk):
                here = slice(s * part_width + start, s * part_width + start + chunk)
                first = s * part + start // head_dim
                heads = slice(first, first + chunk_heads)
                v = got_d[k, :, here].T.astype(F32) * over_rows(got_w[k, heads, :], head_dim)
                v = v * scale_rows[here, :]
                v_parts = jnp.concatenate(split(v), axis=1)
                parts_ref[start : start + chunk, lanes] = v_parts
                d_c += dot(codes_flip[:, here], v_parts)
                out_dl[k, heads, :] = head_sums(v * dot(codes_ref[here, :], c_flip), head_dim)
            out_dc[k, :, s * state_dim : (s + 1) * state_dim] = (d_c[:, :tok] + d_c[:, tok:]).T

            @pl.when(k > 0)
            def _():
                back_dc(k, s).start()
                back_dl(k, s).start()

            c_twice[lanes, :] = jnp.concatenate([c, c], axis=0)
            return carry

        lax.fori_loop(0, count, one_response, 0)

        def one_chunk(j, carry, s=s):
            rows = pl.ds(pl.multiple_of(j * chunk, chunk), chunk)
            here = pl.ds(pl.multiple_of(s * part_width + j * chunk, chunk), chunk)
            inverse = 1.0 / scale_rows[here, :]
            wide = jnp.concatenate([inverse] * (state_dim // tok), axis=1)
            state_ref[here, :] = dot(parts_ref[rows, :], c_twice[...]) * wide
            return carry

        lax.fori_loop(0, part_width // chunk, one_chunk, 0)
        rows = pl.ds(s * part_width, part_width)
        write = pltpu.make_async_copy(state_ref.at[rows, :], state_hbm.at[rows, :], state_sem.at[s])
        write.start()
        writes.append(write)

    def add_back(owner, d_c, d_l):
        states = state_columns(owner)
        total_ref[:, states] = total_ref[:, states] + d_c
        log_ref[heads_of(owner), :] = d_l

    add_back(me, out_dc[0], out_dl[0])
    for k in range(1, count):
        for s in range(span):
            back_dc(k, s).wait_recv()
            back_dl(k, s).wait_recv()
        add_back(other(k), got_dc[k], got_dl[k])
    gc_ref[...] = total_ref[...].astype(BF16)
    col = col_ref[...]
    d_log = (log_ref[...] + (row_ref[...] - col)).T
    later = dot(jnp.concatenate([upper] * 3, axis=1), three_rows(d_log))
    gdt_ref[...] = (col.T / step - rate * later) / (1.0 + jnp.exp(-dt))

    for k in range(1, count):
        send_w(k).wait_send()
        send_c(k).wait_send()
        for s in range(span):
            send_d(k, s).wait_send()
            back_dc(k, s).wait_send()
            back_dl(k, s).wait_send()
    for write in writes:
        write.wait()


PIECES = 8


def copy_kernel(*refs):
    sources, targets, staged = refs[:4], refs[4:8], refs[8:12]
    in_sem, out_sem = refs[12:]
    rows = sources[0].shape[0] // PIECES
    pieces = [(0, pl.ds(i * rows, rows)) for i in range(PIECES)]
    pieces += [(i, pl.ds(0, sources[i].shape[0])) for i in range(1, 4)]
    loads, stores = [], []
    for n, (i, here) in enumerate(pieces):
        held = staged[i].at[here, :]
        loads.append(pltpu.make_async_copy(sources[i].at[here, :], held, in_sem.at[n]))
        stores.append(pltpu.make_async_copy(held, targets[i].at[here, :], out_sem.at[n]))
    for load in loads:
        load.start()
    for load, store in zip(loads, stores):
        load.wait()
        store.start()
    for store in stores:
        store.wait()


def copied(*results):
    there = pl.BlockSpec(memory_space=pl.ANY)
    return pl.pallas_call(
        copy_kernel,
        in_specs=[there] * 4,
        out_specs=[there] * 4,
        out_shape=[jax.ShapeDtypeStruct(result.shape, result.dtype) for result in results],
        scratch_shapes=[pltpu.VMEM(result.shape, result.dtype) for result in results]
        + [pltpu.SemaphoreType.DMA((PIECES + 3,))] * 2,
        compiler_params=pltpu.CompilerParams(vmem_limit_bytes=VMEM_BYTES),
        name="copy_results",
    )(*results)


def per_device(
    count,
    inputs,
    cotangent,
    b_proj,
    c_proj,
    dt_raw,
    decay_rate,
    state_codes,
    state_scales,
    sign_bucket,
    adv_scale,
    lengths,
):
    x, d, b, c, dt = inputs[0], cotangent[0], b_proj[0], c_proj[0], dt_raw[0]
    tok, all_heads = dt.shape
    own, head_dim, state_dim = state_codes.shape
    groups = b.shape[1] // state_dim
    span = max(1, own * groups // all_heads)
    part = own // span
    width = own * head_dim
    whole = pl.BlockSpec(memory_space=pltpu.VMEM)
    there = pl.BlockSpec(memory_space=pl.ANY)
    scalar = pl.BlockSpec(memory_space=pltpu.SMEM)
    dma = pltpu.SemaphoreType.DMA
    flops = 24 * tok * tok * x.shape[1] + 12 * count * tok * width * state_dim
    results = pl.pallas_call(
        functools.partial(kernel, count, groups, head_dim),
        in_specs=[there, there, whole, whole, whole, whole, there, whole, scalar, scalar, scalar],
        out_specs=[there, whole, whole, whole],
        out_shape=[
            jax.ShapeDtypeStruct((width, state_dim), F32),
            jax.ShapeDtypeStruct(b.shape, BF16),
            jax.ShapeDtypeStruct(c.shape, BF16),
            jax.ShapeDtypeStruct(dt.shape, F32),
        ],
        scratch_shapes=[
            pltpu.VMEM(x.shape, BF16),
            pltpu.VMEM(d.shape, BF16),
            pltpu.VMEM((width, state_dim), BF16),
            pltpu.VMEM((width, state_dim), F32),
            pltpu.VMEM((count, tok, width), BF16),
            pltpu.VMEM((count, tok, span * state_dim), BF16),
            pltpu.VMEM((count, own, tok), F32),
            pltpu.VMEM((part * head_dim, count * 2 * tok), BF16),
            pltpu.VMEM((count * 2 * tok, state_dim), BF16),
            pltpu.VMEM((state_dim, width), BF16),
            pltpu.VMEM((width, tok), F32),
            pltpu.VMEM((count, tok, span * state_dim), F32),
            pltpu.VMEM((count, own, tok), F32),
            pltpu.VMEM((count, tok, span * state_dim), F32),
            pltpu.VMEM((count, own, tok), F32),
        ]
        + [pltpu.VMEM((all_heads, tok), F32)] * 5
        + [pltpu.VMEM(c.shape, F32), dma((4,)), dma((span,))]
        + [dma((count, span))] * 2
        + [dma((count,))] * 4
        + [dma((count, span))] * 4,
        compiler_params=pltpu.CompilerParams(
            collective_id=0, has_side_effects=True, vmem_limit_bytes=VMEM_BYTES
        ),
        cost_estimate=pl.CostEstimate(
            flops=flops, bytes_accessed=4 * x.size + 8 * width * state_dim, transcendentals=0
        ),
        name="scan_backward",
    )(
        x,
        d,
        b,
        c,
        dt,
        decay_rate.reshape(1, all_heads),
        state_codes.reshape(width, state_dim),
        state_scales,
        sign_bucket,
        adv_scale,
        lengths,
    )
    grad_state, grad_b, grad_c, grad_dt = copied(*results)
    return grad_state.reshape(state_codes.shape), grad_b[None], grad_c[None], grad_dt[None]


def solution(mesh):
    both = ("prompt", "resp")
    return jax.shard_map(
        functools.partial(per_device, mesh.shape["resp"]),
        mesh=mesh,
        in_specs=(
            P(both, None, None),
            P(both, None, None),
            P(both, None, None),
            P(both, None, None),
            P(both, None, None),
            P(),
            P(both, None, None),
            P(both, None),
            P(both),
            P(both),
            P(both),
        ),
        out_specs=(P(both, None, None),) * 4,
        check_vma=False,
    )
```

```python
import functools
import jax
import jax.numpy as jnp
from jax import lax
from jax.experimental import pallas as pl
from jax.experimental.pallas import tpu as pltpu
from jax.sharding import PartitionSpec as P

F32 = jnp.float32
BF16 = jnp.bfloat16
CHUNK = 512
VMEM_BYTES = 56 * 1024 * 1024


def dot(left, right):
    return lax.dot_general(left, right, (((1,), (0,)), ((), ())), preferred_element_type=F32)


def dot_nt(left, right):
    return lax.dot_general(left, right, (((1,), (1,)), ((), ())), preferred_element_type=F32)


def dot_tn(left, right):
    return lax.dot_general(left, right, (((0,), (0,)), ((), ())), preferred_element_type=F32)


def split(value):
    high = value.astype(BF16)
    return high, (value - high.astype(F32)).astype(BF16)


def three_rows(value):
    high = value.astype(BF16)
    middle, low = split(value - high.astype(F32))
    return jnp.concatenate([high, middle, low], axis=0)


def over_rows(weights, head_dim):
    heads, tok = weights.shape
    return jnp.broadcast_to(weights[:, None, :], (heads, head_dim, tok)).reshape(-1, tok)


def head_sums(value, head_dim):
    rows, tok = value.shape
    return jnp.sum(value.reshape(rows // head_dim, head_dim, tok), axis=1)


def kernel(
    count,
    groups,
    head_dim,
    x_hbm,
    d_hbm,
    b_ref,
    c_ref,
    dt_ref,
    rate_ref,
    codes_hbm,
    scale_ref,
    sign_ref,
    adv_ref,
    length_ref,
    state_hbm,
    gb_ref,
    gc_ref,
    gdt_ref,
    x_ref,
    d_ref,
    codes_ref,
    state_ref,
    got_d,
    got_c,
    got_w,
    parts_ref,
    c_twice,
    codes_flip,
    scale_rows,
    out_dc,
    out_dl,
    got_dc,
    got_dl,
    wa_ref,
    wb_ref,
    row_ref,
    col_ref,
    log_ref,
    total_ref,
    load_sem,
    state_sem,
    d_send,
    d_recv,
    c_send,
    c_recv,
    w_send,
    w_recv,
    dc_send,
    dc_recv,
    dl_send,
    dl_recv,
):
    tok, all_heads = dt_ref.shape
    state_dim = b_ref.shape[1] // groups
    group_heads = all_heads // groups
    group_width = group_heads * head_dim
    own = all_heads // count
    width = own * head_dim
    span = max(1, own // group_heads)
    part = own // span
    part_width = part * head_dim
    me = lax.axis_index("resp")

    def other(k):
        return lax.rem(me + k + count, count)

    def first_group(owner):
        return owner * own // group_heads

    barrier = pltpu.get_barrier_semaphore()
    for k in range(1, count):
        pl.semaphore_signal(
            barrier, inc=1, device_id={"resp": other(k)}, device_id_type=pl.DeviceIdType.MESH
        )

    def columns(owner, s):
        return pl.ds(pl.multiple_of(owner * width + s * part_width, 128), part_width)

    loads = [
        pltpu.make_async_copy(x_hbm, x_ref, load_sem.at[0]),
        pltpu.make_async_copy(d_hbm, d_ref, load_sem.at[1]),
        pltpu.make_async_copy(codes_hbm, codes_ref, load_sem.at[2]),
        pltpu.make_async_copy(
            d_hbm.at[:, pl.ds(pl.multiple_of(me * width, 128), width)], got_d.at[0], load_sem.at[3]
        ),
    ]
    for load in loads:
        load.start()
    pl.semaphore_wait(barrier, count - 1)

    def remote(source, target, send, recv, k):
        return pltpu.make_async_remote_copy(
            src_ref=source,
            dst_ref=target,
            send_sem=send,
            recv_sem=recv,
            device_id={"resp": other(k)},
            device_id_type=pl.DeviceIdType.MESH,
        )

    last = span - 1
    half = tok // 2
    steps = [(s, 0, tok) for s in range(last)] + [(last, 0, half), (last, half, half)]

    def send_d(k, n):
        s, first, rows = steps[n]
        return remote(
            d_hbm.at[pl.ds(first, rows), columns(other(k), s)],
            got_d.at[k, pl.ds(first, rows), pl.ds(s * part_width, part_width)],
            d_send.at[k, n],
            d_recv.at[k, n],
            k,
        )

    def state_columns(owner):
        return pl.ds(pl.multiple_of(first_group(owner) * state_dim, 128), span * state_dim)

    def heads_of(owner):
        return pl.ds(pl.multiple_of(owner * own, 8), own)

    def send_c(k):
        return remote(
            c_ref.at[:, state_columns(other(k))], got_c.at[k], c_send.at[k], c_recv.at[k], k
        )

    def send_w(k):
        return remote(wa_ref.at[heads_of(other(k)), :], got_w.at[k], w_send.at[k], w_recv.at[k], k)

    for k in range(1, count):
        send_d(k, 0).start()

    at = lax.broadcasted_iota(jnp.int32, (tok, tok), 0)
    of = lax.broadcasted_iota(jnp.int32, (tok, tok), 1)
    causal = at >= of
    lower = jnp.where(causal, 1.0, 0.0).astype(BF16)
    upper = jnp.where(at <= of, 1.0, 0.0).astype(BF16)
    dt = dt_ref[...]
    step = jnp.maximum(dt, 0.0) + jnp.log1p(jnp.exp(-jnp.abs(dt)))
    rate = rate_ref[...]
    log_decay = -rate * dot(jnp.concatenate([lower] * 3, axis=1), three_rows(step))
    sign = 2.0 * jnp.full((tok, 1), sign_ref[0], jnp.int32).astype(F32) - 1.0
    length = jnp.full((tok, 1), length_ref[0], jnp.int32)
    coefficient = sign * adv_ref[0] / length.astype(F32)
    row_coef = jnp.where(lax.broadcasted_iota(jnp.int32, (tok, 1), 0) < length, coefficient, 0.0)
    wa_ref[...] = (row_coef * jnp.exp(log_decay)).T
    wb_ref[...] = (step * jnp.exp(-log_decay)).T

    for k in range(1, count):
        send_w(k).start()
        send_c(k).start()
    for n in range(1, len(steps)):
        for k in range(1, count):
            send_d(k, n).start()
    got_c[0] = c_ref[:, state_columns(me)]
    got_w[0] = wa_ref[heads_of(me), :]
    loads[0].wait()
    loads[1].wait()

    chunk = min(CHUNK, group_width)
    chunk_heads = chunk // head_dim
    nothing = jnp.zeros((tok, tok), BF16)

    def paired(high, low):
        return jnp.concatenate(
            [jnp.concatenate([high, low], axis=1), jnp.concatenate([high, nothing], axis=1)], axis=0
        )

    def one_group(g, carry):
        states = pl.ds(pl.multiple_of(g * state_dim, 128), state_dim)
        b = b_ref[:, states]
        c = c_ref[:, states]
        scores = paired(*split(jnp.where(causal, dot_nt(c, b), 0.0)))
        flipped = paired(*split(jnp.where(at <= of, dot_nt(b, c), 0.0)))
        d_scores = jnp.zeros((2 * tok, 2 * tok), F32)
        for start in range(0, group_width, chunk):
            here = pl.ds(pl.multiple_of(g * group_width + start, 128), chunk)
            heads = pl.ds(
                pl.multiple_of(g * group_heads + start // head_dim, chunk_heads), chunk_heads
            )
            w = d_ref[:, here].T.astype(F32) * over_rows(wa_ref[heads, :], head_dim)
            x = x_ref[:, here].T.astype(F32) * over_rows(wb_ref[heads, :], head_dim)
            w_parts = jnp.concatenate(split(w), axis=1)
            x_parts = jnp.concatenate(split(x), axis=1)
            d_scores += dot_tn(w_parts, x_parts)
            y = dot(x_parts, flipped)
            u = dot(w_parts, scores)
            row_ref[heads, :] = head_sums(w * (y[:, :tok] + y[:, tok:]), head_dim)
            col_ref[heads, :] = head_sums(x * (u[:, :tok] + u[:, tok:]), head_dim)
        d_scores = d_scores[:tok] + d_scores[tok:]
        d_scores = jnp.where(causal, d_scores[:, :tok] + d_scores[:, tok:], 0.0)
        total_ref[:, states] = dot(
            jnp.concatenate(split(d_scores), axis=1), jnp.concatenate([b, b], axis=0)
        )
        gb_ref[:, states] = dot(
            jnp.concatenate(split(d_scores.T), axis=1), jnp.concatenate([c, c], axis=0)
        ).astype(BF16)
        return carry

    lax.fori_loop(0, groups, one_group, 0)

    loads[2].wait()
    loads[3].wait()
    chunk = min(CHUNK, part_width)
    chunk_heads = chunk // head_dim
    scales = scale_ref[...].astype(F32).T
    for h in range(own):
        scale_rows[h * head_dim : (h + 1) * head_dim, :] = jnp.broadcast_to(
            scales[:, h : h + 1], (head_dim, tok)
        )
    for start in range(0, width, chunk):
        codes_flip[:, start : start + chunk] = codes_ref[start : start + chunk, :].T

    def back_dc(k, n):
        s, first, rows = steps[n]
        return remote(
            out_dc.at[k, pl.ds(first, rows), pl.ds(s * state_dim, state_dim)],
            got_dc.at[k, pl.ds(first, rows), pl.ds(s * state_dim, state_dim)],
            dc_send.at[k, n],
            dc_recv.at[k, n],
            -k,
        )

    def back_dl(k, s):
        return remote(
            out_dl.at[k, pl.ds(s * part, part), :],
            got_dl.at[k, pl.ds(s * part, part), :],
            dl_send.at[k, s],
            dl_recv.at[k, s],
            -k,
        )

    writes = []

    def from_state(k, s, first, rows):
        tokens = slice(first, first + rows)
        lanes = pl.ds(pl.multiple_of(k * 2 * tok + 2 * first, 128), 2 * rows)
        c = got_c[k, tokens, s * state_dim : (s + 1) * state_dim]
        c_flip = c.T
        d_c = jnp.zeros((state_dim, 2 * rows), F32)
        for start in range(0, part_width, chunk):
            here = slice(s * part_width + start, s * part_width + start + chunk)
            head = s * part + start // head_dim
            heads = slice(head, head + chunk_heads)
            v = got_d[k, tokens, here].T.astype(F32) * over_rows(got_w[k, heads, tokens], head_dim)
            v = v * scale_rows[here, :rows]
            v_parts = jnp.concatenate(split(v), axis=1)
            parts_ref[start : start + chunk, lanes] = v_parts
            d_c += dot(codes_flip[:, here], v_parts)
            out_dl[k, heads, tokens] = head_sums(v * dot(codes_ref[here, :], c_flip), head_dim)
        out_dc[k, tokens, s * state_dim : (s + 1) * state_dim] = (d_c[:, :rows] + d_c[:, rows:]).T
        c_twice[lanes, :] = jnp.concatenate([c, c], axis=0)

    for s in range(span):
        from_state(0, s, 0, tok)
        for n in [n for n in range(len(steps)) if steps[n][0] == s]:

            def one_response(k, carry, n=n, s=s):
                if n == 0:
                    send_w(k).wait_recv()
                    send_c(k).wait_recv()
                send_d(k, n).wait_recv()
                from_state(k, *steps[n])
                back_dc(k, n).start()
                if steps[n][1] + steps[n][2] == tok:
                    back_dl(k, s).start()
                return carry

            lax.fori_loop(1, count, one_response, 0)

        def one_chunk(j, carry, s=s):
            rows = pl.ds(pl.multiple_of(j * chunk, chunk), chunk)
            here = pl.ds(pl.multiple_of(s * part_width + j * chunk, chunk), chunk)
            inverse = 1.0 / scale_rows[here, :]
            wide = jnp.concatenate([inverse] * (state_dim // tok), axis=1)
            state_ref[here, :] = dot(parts_ref[rows, :], c_twice[...]) * wide
            return carry

        lax.fori_loop(0, part_width // chunk, one_chunk, 0)
        rows = pl.ds(s * part_width, part_width)
        write = pltpu.make_async_copy(state_ref.at[rows, :], state_hbm.at[rows, :], state_sem.at[s])
        write.start()
        writes.append(write)

    def add_back(owner, d_c, d_l):
        states = state_columns(owner)
        total_ref[:, states] = total_ref[:, states] + d_c
        log_ref[heads_of(owner), :] = d_l

    add_back(me, out_dc[0], out_dl[0])
    for n, (s, first, rows) in enumerate(steps):
        cols = slice(s * state_dim, (s + 1) * state_dim)
        for k in range(1, count):
            back_dc(k, n).wait_recv()
            begin = pl.multiple_of((first_group(other(k)) + s) * state_dim, 128)
            states = pl.ds(begin, state_dim)
            tokens = slice(first, first + rows)
            total_ref[tokens, states] = total_ref[tokens, states] + got_dc[k, tokens, cols]
            if first + rows == tok:
                back_dl(k, s).wait_recv()
                heads = pl.ds(pl.multiple_of(other(k) * own + s * part, 8), part)
                log_ref[heads, :] = got_dl[k, s * part : (s + 1) * part, :]
    gc_ref[...] = total_ref[...].astype(BF16)
    col = col_ref[...]
    d_log = (log_ref[...] + (row_ref[...] - col)).T
    later = dot(jnp.concatenate([upper] * 3, axis=1), three_rows(d_log))
    gdt_ref[...] = (col.T / step - rate * later) / (1.0 + jnp.exp(-dt))

    for k in range(1, count):
        send_w(k).wait_send()
        send_c(k).wait_send()
        for n in range(len(steps)):
            send_d(k, n).wait_send()
            back_dc(k, n).wait_send()
        for s in range(span):
            back_dl(k, s).wait_send()
    for write in writes:
        write.wait()


PIECES = 8


def copy_kernel(*refs):
    sources, targets, staged = refs[:4], refs[4:8], refs[8:12]
    in_sem, out_sem = refs[12:]
    rows = sources[0].shape[0] // PIECES
    pieces = [(0, pl.ds(i * rows, rows)) for i in range(PIECES)]
    pieces += [(i, pl.ds(0, sources[i].shape[0])) for i in range(1, 4)]
    loads, stores = [], []
    for n, (i, here) in enumerate(pieces):
        held = staged[i].at[here, :]
        loads.append(pltpu.make_async_copy(sources[i].at[here, :], held, in_sem.at[n]))
        stores.append(pltpu.make_async_copy(held, targets[i].at[here, :], out_sem.at[n]))
    for load in loads:
        load.start()
    for load, store in zip(loads, stores):
        load.wait()
        store.start()
    for store in stores:
        store.wait()


def copied(*results):
    there = pl.BlockSpec(memory_space=pl.ANY)
    return pl.pallas_call(
        copy_kernel,
        in_specs=[there] * 4,
        out_specs=[there] * 4,
        out_shape=[jax.ShapeDtypeStruct(result.shape, result.dtype) for result in results],
        scratch_shapes=[pltpu.VMEM(result.shape, result.dtype) for result in results]
        + [pltpu.SemaphoreType.DMA((PIECES + 3,))] * 2,
        compiler_params=pltpu.CompilerParams(vmem_limit_bytes=VMEM_BYTES),
        name="copy_results",
    )(*results)


def per_device(
    count,
    inputs,
    cotangent,
    b_proj,
    c_proj,
    dt_raw,
    decay_rate,
    state_codes,
    state_scales,
    sign_bucket,
    adv_scale,
    lengths,
):
    x, d, b, c, dt = inputs[0], cotangent[0], b_proj[0], c_proj[0], dt_raw[0]
    tok, all_heads = dt.shape
    own, head_dim, state_dim = state_codes.shape
    groups = b.shape[1] // state_dim
    span = max(1, own * groups // all_heads)
    part = own // span
    width = own * head_dim
    whole = pl.BlockSpec(memory_space=pltpu.VMEM)
    there = pl.BlockSpec(memory_space=pl.ANY)
    scalar = pl.BlockSpec(memory_space=pltpu.SMEM)
    dma = pltpu.SemaphoreType.DMA
    flops = 24 * tok * tok * x.shape[1] + 12 * count * tok * width * state_dim
    results = pl.pallas_call(
        functools.partial(kernel, count, groups, head_dim),
        in_specs=[there, there, whole, whole, whole, whole, there, whole, scalar, scalar, scalar],
        out_specs=[there, whole, whole, whole],
        out_shape=[
            jax.ShapeDtypeStruct((width, state_dim), F32),
            jax.ShapeDtypeStruct(b.shape, BF16),
            jax.ShapeDtypeStruct(c.shape, BF16),
            jax.ShapeDtypeStruct(dt.shape, F32),
        ],
        scratch_shapes=[
            pltpu.VMEM(x.shape, BF16),
            pltpu.VMEM(d.shape, BF16),
            pltpu.VMEM((width, state_dim), BF16),
            pltpu.VMEM((width, state_dim), F32),
            pltpu.VMEM((count, tok, width), BF16),
            pltpu.VMEM((count, tok, span * state_dim), BF16),
            pltpu.VMEM((count, own, tok), F32),
            pltpu.VMEM((part * head_dim, count * 2 * tok), BF16),
            pltpu.VMEM((count * 2 * tok, state_dim), BF16),
            pltpu.VMEM((state_dim, width), BF16),
            pltpu.VMEM((width, tok), F32),
            pltpu.VMEM((count, tok, span * state_dim), F32),
            pltpu.VMEM((count, own, tok), F32),
            pltpu.VMEM((count, tok, span * state_dim), F32),
            pltpu.VMEM((count, own, tok), F32),
        ]
        + [pltpu.VMEM((all_heads, tok), F32)] * 5
        + [pltpu.VMEM(c.shape, F32), dma((4,)), dma((span,))]
        + [dma((count, span + 1))] * 2
        + [dma((count,))] * 4
        + [dma((count, span + 1))] * 4,
        compiler_params=pltpu.CompilerParams(
            collective_id=0, has_side_effects=True, vmem_limit_bytes=VMEM_BYTES
        ),
        cost_estimate=pl.CostEstimate(
            flops=flops, bytes_accessed=4 * x.size + 8 * width * state_dim, transcendentals=0
        ),
        name="scan_backward",
    )(
        x,
        d,
        b,
        c,
        dt,
        decay_rate.reshape(1, all_heads),
        state_codes.reshape(width, state_dim),
        state_scales,
        sign_bucket,
        adv_scale,
        lengths,
    )
    grad_state, grad_b, grad_c, grad_dt = copied(*results)
    return grad_state.reshape(state_codes.shape), grad_b[None], grad_c[None], grad_dt[None]


def solution(mesh):
    both = ("prompt", "resp")
    return jax.shard_map(
        functools.partial(per_device, mesh.shape["resp"]),
        mesh=mesh,
        in_specs=(
            P(both, None, None),
            P(both, None, None),
            P(both, None, None),
            P(both, None, None),
            P(both, None, None),
            P(),
            P(both, None, None),
            P(both, None),
            P(both),
            P(both),
            P(both),
        ),
        out_specs=(P(both, None, None),) * 4,
        check_vma=False,
    )
```
